128 devices in a mesh: section: 2 (over x_hi), replica: 4 (over y), shard: 16 (over x_lo, z, core).
Axes of the slice: x: 4 (x_hi: 2, x_lo: 2; x = x_hi * 2 + x_lo), y: 4, z: 4, core: 2. Of those that a mesh axis runs over, the one named last changes fastest.
Arguments:
- inputs: bfloat16 [2, 64, 197, 768], P(None, ('replica', 'shard')), may hold values from -6 to 6
- cotangent: bfloat16 [2, 64, 197, 768], P(None, ('replica', 'shard')), may hold values from -6 to 6
- routes: int32 [2, 2, 64, 197, 2], P('section', None, ('replica', 'shard')), may hold values from 0 to 2, all different within a row
- norm_gain: bfloat16 [2, 2, 768], P('section', None, 'shard'), may hold values from 0.5 to 1.5
- norm_offset: bfloat16 [2, 2, 768], P('section', None, 'shard'), may hold values from -0.5 to 0.5
- w_qkv: bfloat16 [2, 768, 2304], P('section', 'shard'), may hold values from -0.21875 to 0.21875
- w_proj: bfloat16 [2, 768, 768], P('section', 'shard'), may hold values from -3.5 to 3.5
- w_router: bfloat16 [2, 768, 3], P('section', 'shard'), may hold values from -0.15625 to 0.15625
- experts_in: bfloat16 [2, 3072, 3, 768], P('section', 'shard'), may hold values from -0.21875 to 0.21875
- experts_out: bfloat16 [2, 3072, 3, 768], P('section', 'shard'), may hold values from -0.3125 to 0.3125
Outputs:
- section_out: bfloat16 [2, 2, 64, 197, 768], P('section', None, ('replica', 'shard'))
- section_in_grad: float32 [2, 2, 64, 197, 768], P('section', None, ('replica', 'shard'))
- grad_gain: float32 [2, 2, 768], P('section', None, 'shard')
- grad_offset: float32 [2, 2, 768], P('section', None, 'shard')
- grad_qkv: float32 [2, 768, 2304], P('section', 'shard')
- grad_proj: float32 [2, 768, 768], P('section', 'shard')
- grad_router: float32 [2, 768, 3], P('section', 'shard')
- grad_in: float32 [2, 3072, 3, 768], P('section', 'shard')
- grad_out: float32 [2, 3072, 3, 768], P('section', 'shard')
The draws below stay inside these ranges and needn't reach their ends.
Inputs may be any that keep to these rules, and one draw needn't show every extreme that they name: `routes`: each token names two different experts of the 3, its preferred one first.
All inputs are finite; a program needn't handle non-finite values.
Results may differ from the reference program's by a relative error of at most 0.03.
Values may be sent and summed in bfloat16 or wider, within the bound.
A program may use at most 256 MiB of HBM per device.

```python
import jax
import jax.numpy as jnp
from jax import lax

D = 768
HEADS = 12
HEAD_DIM = 64
FF = 3072
SEQ = 197
EXPERTS = 3
MICRO = 2
IMG_DEV = 1
SECTIONS = 2
IMAGES = 64
CAPACITY = 72


def levels(rng, shape, shards, least, high):
    factor_of = 1.0
    for dim, shards_of in shards:
        steps = jax.random.uniform(jax.random.fold_in(jax.random.fold_in(rng, 6), dim), (shards_of,), jnp.float32, least / len(shards), high / len(shards))
        factor_of = factor_of * jnp.repeat(jnp.exp(steps), shape[dim] // shards_of).reshape((-1,) + (1,) * (len(shape) - 1 - dim))
    return factor_of


def choose_distinct(own_key, rows, number_of, top, lift):
    order = jax.random.permutation(jax.random.fold_in(own_key, 1), number_of)
    favour = order
    for power in range(3):
        favour = favour * favour // number_of
    favour = favour * lift // number_of
    chance = jax.random.randint(jax.random.fold_in(own_key, 2), (rows, number_of), 0, 4096) + favour
    sure = jax.random.permutation(jax.random.fold_in(own_key, 3), rows)[jnp.arange(number_of) % rows]
    chance = jnp.where(jnp.arange(rows)[:, None] == sure[None, :], 1 << 14, chance)
    merit = chance * number_of + jnp.arange(number_of)
    return lax.top_k(merit.astype(jnp.int32), top)[1].astype(jnp.int32)


def normal_values(rng, extent, scale, most, cuts=(), held_as=jnp.bfloat16):
    values = scale * jax.random.normal(rng, extent, jnp.float32)
    if cuts:
        values = values * levels(rng, extent, cuts, -0.22, 0.18)
    return jnp.clip(values, -most, most).astype(held_as)


def setup_inputs(seed: int = 0) -> dict:
    key_of = jax.random.split(jax.random.key(seed), 11)
    return {
        "inputs": normal_values(key_of[0], (MICRO, IMAGES, SEQ, D), 1.0, 6.0, ((1, 64),)),
        "cotangent": normal_values(key_of[1], (MICRO, IMAGES, SEQ, D), 1.0, 6.0, ((1, 64),)),
        "routes": choose_distinct(key_of[2], SECTIONS * MICRO * IMAGES * SEQ, EXPERTS, 2, 5461).reshape((SECTIONS, MICRO, IMAGES, SEQ, 2)),
        "norm_gain": jnp.clip(1.0 + 0.1 * jax.random.normal(key_of[3], (SECTIONS, 2, D), jnp.float32), 0.5, 1.5).astype(jnp.bfloat16),
        "norm_offset": normal_values(key_of[4], (SECTIONS, 2, D), 0.1, 0.5, ((0, 2), (2, 16))),
        "w_qkv": normal_values(key_of[5], (SECTIONS, D, 3 * D), D ** -0.5, 0.21875, ((0, 2), (1, 16))),
        "w_proj": normal_values(key_of[6], (SECTIONS, D, D), (D // SEQ) ** -0.5, 3.5, ((0, 2), (1, 16))),
        "w_router": normal_values(key_of[7], (SECTIONS, D, EXPERTS), (2 * D) ** -0.5, 0.15625, ((0, 2), (1, 16))),
        "experts_in": normal_values(key_of[8], (SECTIONS, FF, EXPERTS, D), D ** -0.5, 0.21875, ((0, 2), (1, 16))),
        "experts_out": normal_values(key_of[9], (SECTIONS, FF, EXPERTS, D), (FF // 8) ** -0.5, 0.3125, ((0, 2), (1, 16))),
    }


@jax.custom_vjp
def low(v):
    return lax.optimization_barrier(v.astype(jnp.bfloat16)).astype(jnp.float32)

@jax.custom_vjp
def low_back(v):
    return v

def low_keep(v):
    return (low(v), None)

def low_pass(kept, grad):
    return (grad,)

def back_keep(v):
    return (v, None)

def back_low(kept, grad):
    return (low(grad),)
low.defvjp(low_keep, low_pass)
low_back.defvjp(back_keep, back_low)
EPSILON = 1e-06
HIGHEST = lax.Precision.HIGHEST

def both_ways(value):
    return low(low_back(value))

def norm_rows(values, gain_row, offset_row):
    centre = values - lax.optimization_barrier(jnp.mean(values, axis=-1, keepdims=True))
    spread = lax.optimization_barrier(jnp.mean(centre * centre, axis=-1, keepdims=True))
    return centre * lax.rsqrt(spread + EPSILON) * gain_row + offset_row

def soft_rows(scores):
    largest = lax.optimization_barrier(jnp.max(scores, axis=-1, keepdims=True))
    expo_rows = jnp.exp(scores - largest)
    return expo_rows / lax.optimization_barrier(jnp.sum(expo_rows, axis=-1, keepdims=True))

def attend_image(blocks):
    queries, key_rows, value_rows = blocks
    scores = low_back(jnp.einsum('qhd,khd->hqk', queries, key_rows, precision=HIGHEST) * HEAD_DIM ** (-0.5))
    probs_low = low(soft_rows(scores))
    return jnp.einsum('hqk,khd->qhd', probs_low, value_rows, precision=HIGHEST)

def expert_block(normed, gate_rows, picked_ids, experts_in, experts_out):
    row_count = normed.shape[0]
    picked = jnp.concatenate([picked_ids[:, 0], picked_ids[:, 1]])
    pick_hot = (picked[:, None] == jnp.arange(EXPERTS, dtype=jnp.int32)[None, :]).astype(jnp.int32)
    before = jnp.cumsum(pick_hot, axis=0) - pick_hot
    position = lax.optimization_barrier(jnp.sum(before * pick_hot, axis=1))
    slot_ids = jnp.where(position < CAPACITY, position * EXPERTS + picked, CAPACITY * EXPERTS).astype(jnp.int32)
    row_pairs = jnp.concatenate([normed, normed], axis=0)
    slot_rows = jnp.zeros((CAPACITY * EXPERTS + 1, D), jnp.float32).at[slot_ids].set(row_pairs)
    slot_in = slot_rows[:-1].reshape(CAPACITY, EXPERTS, D)
    pre_rows = low_back(jnp.einsum('ced,red->cer', slot_in, experts_in, precision=HIGHEST))
    hidden = low(jax.nn.gelu(pre_rows))
    result = both_ways(jnp.einsum('cer,red->ced', hidden, experts_out, precision=HIGHEST))
    padded = jnp.concatenate([result.reshape(CAPACITY * EXPERTS, D), jnp.zeros((1, D), jnp.float32)], axis=0)
    taken_rows = padded[slot_ids]
    gate_pair = jnp.take_along_axis(gate_rows, picked_ids, axis=1)
    return taken_rows[:row_count] * gate_pair[:, 0:1] + taken_rows[row_count:] * gate_pair[:, 1:2]

def layer(inputs, gain_pair, offset_pair, w_qkv, w_proj, w_router, experts_in, experts_out, picked_ids):
    images = inputs.shape[0]
    normed_in = low(norm_rows(inputs, gain_pair[0], offset_pair[0]))
    projected = both_ways(jnp.einsum('isd,de->ise', normed_in, w_qkv, precision=HIGHEST))
    split_qkv = projected.reshape(images, SEQ, 3, HEADS, HEAD_DIM)
    attended = lax.map(jax.checkpoint(attend_image), (split_qkv[:, :, 0], split_qkv[:, :, 1], split_qkv[:, :, 2]))
    mixed_low = both_ways(attended.reshape(images, SEQ, D))
    residual = inputs + low_back(jnp.einsum('isd,de->ise', mixed_low, w_proj, precision=HIGHEST))
    normed = low(norm_rows(residual, gain_pair[1], offset_pair[1]))
    logits = low_back(jnp.einsum('isd,de->ise', normed, w_router, precision=HIGHEST))
    gate_rows = soft_rows(logits)
    devices = images // IMG_DEV
    tok_dev = IMG_DEV * SEQ

    def route_block(pieces):
        return expert_block(pieces[0], pieces[1], pieces[2], experts_in, experts_out)
    expert_sum = lax.map(jax.checkpoint(route_block), (normed.reshape(devices, tok_dev, D), gate_rows.reshape(devices, tok_dev, EXPERTS), picked_ids.reshape(devices, tok_dev, 2)))
    return residual + expert_sum.reshape(images, SEQ, D)

def reference(inputs, cotangent, routes, norm_gain, norm_offset, w_qkv, w_proj, w_router, experts_in, experts_out):
    params = tuple((weight.astype(jnp.float32) for weight in (norm_gain, norm_offset, w_qkv, w_proj, w_router, experts_in, experts_out)))
    start_in = inputs.astype(jnp.float32)
    shifts = jnp.zeros((SECTIONS,) + inputs.shape, jnp.float32)

    def forward(params, shifts):
        table_rows = [[None] * MICRO for section_at in range(SECTIONS)]
        for micro_at in range(MICRO):
            current = start_in[micro_at]
            for section_at in range(SECTIONS):
                current = layer(current + shifts[section_at, micro_at], *[weight[section_at] for weight in params], routes[section_at, micro_at])
                if section_at + 1 < SECTIONS:
                    current = both_ways(current)
                table_rows[section_at][micro_at] = current
        return jnp.stack([jnp.stack(row_list) for row_list in table_rows])
    section_outs, pull_back = jax.vjp(forward, params, shifts)
    out_cotangent = jnp.concatenate([jnp.zeros((SECTIONS - 1,) + inputs.shape, jnp.float32), cotangent.astype(jnp.float32)[None]], axis=0)
    param_grads, shift_grads = pull_back(out_cotangent)
    return (section_outs.astype(jnp.bfloat16), shift_grads, param_grads[0], param_grads[1], param_grads[2], param_grads[3], param_grads[4], param_grads[5], param_grads[6])
```

```python
import jax
import jax.numpy as jnp
from jax import lax
from jax.experimental import pallas as pl
from jax.experimental.pallas import tpu as pltpu
from jax.sharding import PartitionSpec as P

MESH = pl.DeviceIdType.MESH

def place():
    j = lax.axis_index("shard")
    return j // 8, (j // 2) % 4, j % 2, lax.axis_index("replica")

def at_shard(xl, z, c):
    return {"shard": xl * 8 + z * 2 + c}

class Copies:
    def __init__(self, send, recv):
        self.send, self.recv, self.n, self.all = send, recv, 0, []
    def __call__(self, src, dst, dev):
        cp = pltpu.make_async_remote_copy(src_ref=src, dst_ref=dst, send_sem=self.send.at[self.n], recv_sem=self.recv.at[self.n], device_id=dev, device_id_type=MESH)
        self.n += 1
        cp.start()
        self.all.append(cp)
        return cp

def greet(devs):
    b = pltpu.get_barrier_semaphore()
    for d in devs:
        pl.semaphore_signal(b, inc=1, device_id=d, device_id_type=MESH)
    pl.semaphore_wait(b, len(devs))

def halves(n):
    half = n // 32 * 16
    return (half, n - half)


def gather_kernel(p_rows, q_rows, core, own, out, send, recv, loc):
    xl, z, c, y = place()
    ox, zu, zd, zo = 1 - xl, (z + 1) % 4, (z + 3) % 4, (z + 2) % 4
    yu, yd, yo = (y + 1) % 4, (y + 3) % 4, (y + 2) % 4
    dx, du, dd, dc = at_shard(ox, z, c), at_shard(xl, zu, c), at_shard(xl, zd, c), at_shard(xl, z, 1 - c)
    dyu, dyd = {"replica": yu}, {"replica": yd}
    greet([dx, du, dd, dyu, dyd] + ([dc] if core else []))
    go = Copies(send, recv)
    n = q_rows // 4
    def quarter(k):
        return pl.ds(pl.multiple_of(p_rows + k * n, 16), n)
    def lower(k):
        return pl.ds(pl.multiple_of(p_rows + k * n, 16), halves(n)[0])
    def upper(k):
        return pl.ds(pl.multiple_of(p_rows + k * n + halves(n)[0], 16), halves(n)[1])
    def block(a, b, rows):
        return out.at[a, b, c, rows]
    def pass_on(a, b, rows, dev):
        return go(block(a, b, rows), block(a, b, rows), dev)
    cores = []
    def share(a, b, rows):
        if core:
            cores.append(pass_on(a, b, rows, dc))
    local = pltpu.make_async_copy(own, out.at[xl, z, c], loc)
    local.start()
    mine = quarter(y)
    first = pl.ds(0, p_rows)
    plo, pup = pl.ds(0, halves(p_rows)[0]), pl.ds(halves(p_rows)[0], halves(p_rows)[1])
    def from_own(rows, dev):
        return go(own.at[rows], block(xl, z, rows), dev)
    q_up, q_down, q_over = from_own(mine, du), from_own(mine, dd), from_own(mine, dx)
    p_over = from_own(first, dx)
    p_up, p_down = from_own(first, du), from_own(first, dd)
    q_over.wait_recv()
    q_over_up, q_over_down = pass_on(ox, z, mine, du), pass_on(ox, z, mine, dd)
    spread = []
    def over_y(a, b):
        spread.append((a, b, pass_on(a, b, mine, dyu), pass_on(a, b, mine, dyd)))
    q_up.wait_recv()
    f1 = pass_on(xl, zd, lower(y), du)
    over_y(xl, zd)
    q_down.wait_recv()
    f2 = pass_on(xl, zu, upper(y), dd)
    over_y(xl, zu)
    if core:
        cores.append(go(own, out.at[xl, z, c], dc))
    rest_over = [from_own(quarter(k), dx) for k in (yu, yd, yo)]
    q_over_up.wait_recv()
    f3 = pass_on(ox, zd, lower(y), du)
    over_y(ox, zd)
    q_over_down.wait_recv()
    f4 = pass_on(ox, zu, upper(y), dd)
    over_y(ox, zu)
    p_over.wait_recv()
    p_over_up, p_over_down = pass_on(ox, z, first, du), pass_on(ox, z, first, dd)
    f1.wait_recv()
    f2.wait_recv()
    over_y(xl, zo)
    f3.wait_recv()
    f4.wait_recv()
    over_y(ox, zo)
    for a, b in ((xl, zd), (xl, zu), (ox, zd), (ox, zu), (xl, zo), (ox, zo)):
        share(a, b, mine)
    p_up.wait_recv()
    g1 = pass_on(xl, zd, plo, du)
    p_down.wait_recv()
    g2 = pass_on(xl, zu, pup, dd)
    share(xl, zd, first)
    share(xl, zu, first)
    fy = []
    def y_forward(item):
        a, b, up, down = item
        up.wait_recv()
        one = pass_on(a, b, lower(yd), dyu)
        share(a, b, quarter(yd))
        down.wait_recv()
        two = pass_on(a, b, upper(yu), dyd)
        share(a, b, quarter(yu))
        fy.append((a, b, one, two))
    for item in spread[:2]:
        y_forward(item)
    p_over_up.wait_recv()
    g3 = pass_on(ox, zd, plo, du)
    p_over_down.wait_recv()
    g4 = pass_on(ox, zu, pup, dd)
    share(ox, zd, first)
    share(ox, zu, first)
    for item in spread[2:]:
        y_forward(item)
    for cp in rest_over:
        cp.wait_recv()
    share(ox, z, pl.ds(0, p_rows + q_rows))
    for cp in (g1, g2, g3, g4):
        cp.wait_recv()
    share(xl, zo, first)
    share(ox, zo, first)
    for a, b, one, two in fy:
        one.wait_recv()
        two.wait_recv()
        share(a, b, quarter(yo))
    local.wait()
    for cp in cores:
        cp.wait_recv()
    for cp in go.all:
        cp.wait_send()


def gather(own, p_rows, core=True, cid=0):
    r, w = own.shape
    nmax = 80
    def body(own_ref, out_ref, send, recv, loc):
        gather_kernel(p_rows, r - p_rows, core, own_ref, out_ref, send, recv, loc)
    return pl.pallas_call(
        body,
        out_shape=jax.ShapeDtypeStruct((2, 4, 2, r, w), own.dtype),
        in_specs=[pl.BlockSpec(memory_space=pl.ANY)],
        out_specs=pl.BlockSpec(memory_space=pl.ANY),
        scratch_shapes=[pltpu.SemaphoreType.DMA((nmax,)), pltpu.SemaphoreType.DMA((nmax,)), pltpu.SemaphoreType.DMA(())],
        compiler_params=pltpu.CompilerParams(collective_id=cid, has_side_effects=True),
    )(own)


def reduce_kernel(gexp, gden, out, acc, rc, ryh, ryf, rzh, rzf, rx, rfh, rff, small, send, recv, loc):
    xl, z, c, y = place()
    ox, zu, zd, zo = 1 - xl, (z + 1) % 4, (z + 3) % 4, (z + 2) % 4
    yu, yd, yo = (y + 1) % 4, (y + 3) % 4, (y + 2) % 4
    dx, du, dd, dc = at_shard(ox, z, c), at_shard(xl, zu, c), at_shard(xl, zd, c), at_shard(xl, z, 1 - c)
    dyu, dyd, dyo = {"replica": yu}, {"replica": yd}, {"replica": yo}
    greet([dx, du, dd, dc, dyu, dyd, dyo])
    go = Copies(send, recv)
    locals_ = []

    def load(src, dst):
        cp = pltpu.make_async_copy(src, dst, loc.at[len(locals_)])
        cp.start()
        locals_.append(cp)
        return cp

    def add(dst, dst_at, src, src_at, n):
        def body(i, carry):
            rows = pl.ds(pl.multiple_of(dst_at + i * 16, 16), 16)
            more = pl.ds(pl.multiple_of(src_at + i * 16, 16), 16)
            dst[rows] = dst[rows] + src[more]
            return carry
        lax.fori_loop(0, n // 16, body, 0)

    blocks = [(ox, zo), (xl, zo), (ox, zu), (xl, zu), (ox, zd), (xl, zd), (ox, z), (xl, z)]
    exp_rows, den_rows = pl.ds(0, 384), pl.ds(384, 80)
    parts = []
    for a, b in blocks:
        parts.append((
            load(gexp.at[a, b, c], acc.at[a, b, exp_rows]),
            load(gden.at[a, b, c], acc.at[a, b, den_rows]),
            go(gexp.at[a, b, 1 - c], rc.at[a, b, exp_rows], dc),
            go(gden.at[a, b, 1 - c], rc.at[a, b, den_rows], dc),
        ))

    def own_sum(t):
        a, b = blocks[t]
        one, two, three, four = parts[t]
        one.wait()
        two.wait()
        three.wait_recv()
        four.wait_recv()
        add(acc.at[a, b], 0, rc.at[a, b], 0, 464)

    def quarter(k):
        return 208 + k * 64

    def rows(at, n):
        return pl.ds(pl.multiple_of(at, 16), n)

    def piece(t, at, n):
        a, b = blocks[t]
        return acc.at[a, b, rows(at, n)]

    y_half, y_full, z_half, z_full = {}, {}, {}, {}
    for t in range(6):
        own_sum(t)
        y_half[t] = (
            go(piece(t, quarter(yo), 32), ryh.at[t, 0], dyu),
            go(piece(t, quarter(yo) + 32, 32), ryh.at[t, 1], dyd),
        )
        if t < 2:
            z_half[t, 0] = (
                go(piece(t, 0, 96), rzh.at[t, 0, pl.ds(0, 96)], du),
                go(piece(t, 96, 112), rzh.at[t, 1, pl.ds(0, 112)], dd),
            )
    for t in range(6):
        a, b = blocks[t]
        y_half[t][0].wait_recv()
        add(acc.at[a, b], quarter(yu), ryh.at[t, 0], 0, 32)
        y_full_up = go(piece(t, quarter(yu), 64), ryf.at[t, 0], dyu)
        y_half[t][1].wait_recv()
        add(acc.at[a, b], quarter(yd) + 32, ryh.at[t, 1], 0, 32)
        y_full[t] = (y_full_up, go(piece(t, quarter(yd), 64), ryf.at[t, 1], dyd))
        if t == 1:
            for x in range(2):
                z_half[x, 0][0].wait_recv()
                add(acc.at[blocks[x][0], zu], 0, rzh.at[x, 0], 0, 96)
                up = go(piece(2 + x, 0, 208), rzf.at[x, 0, pl.ds(0, 208)], du)
                z_half[x, 0][1].wait_recv()
                add(acc.at[blocks[x][0], zd], 96, rzh.at[x, 1], 0, 112)
                z_full[x, 0] = (up, go(piece(4 + x, 0, 208), rzf.at[x, 1, pl.ds(0, 208)], dd))
    own_sum(6)
    own_sum(7)
    for t in range(6):
        a, b = blocks[t]
        for side in range(2):
            y_full[t][side].wait_recv()
            add(acc.at[a, b], quarter(y), ryf.at[t, side], 0, 64)
        if t < 2:
            z_half[t, 1] = (
                go(piece(t, quarter(y), 32), rzh.at[t, 0, pl.ds(112, 32)], du),
                go(piece(t, quarter(y) + 32, 32), rzh.at[t, 1, pl.ds(112, 32)], dd),
            )
    over = []
    for x in range(2):
        for side in range(2):
            z_full[x, 0][side].wait_recv()
            add(acc.at[blocks[x][0], z], 0, rzf.at[x, side], 0, 208)
        if x == 0:
            over.append(go(acc.at[ox, z, pl.ds(0, 208)], rx.at[pl.ds(0, 208)], dx))
        z_half[x, 1][0].wait_recv()
        add(acc.at[blocks[x][0], zu], quarter(y), rzh.at[x, 0], 112, 32)
        up = go(piece(2 + x, quarter(y), 64), rzf.at[x, 0, pl.ds(208, 64)], du)
        z_half[x, 1][1].wait_recv()
        add(acc.at[blocks[x][0], zd], quarter(y) + 32, rzh.at[x, 1], 112, 32)
        z_full[x, 1] = (up, go(piece(4 + x, quarter(y), 64), rzf.at[x, 1, pl.ds(208, 64)], dd))
    for x in range(2):
        for side in range(2):
            z_full[x, 1][side].wait_recv()
            add(acc.at[blocks[x][0], z], quarter(y), rzf.at[x, side], 208, 64)
        if x == 0:
            over.append(go(acc.at[ox, z, pl.ds(208, 256)], rx.at[pl.ds(208, 256)], dx))
    own = acc.at[xl, z]
    over[0].wait_recv()
    add(own, 0, rx, 0, 208)
    over[1].wait_recv()
    add(own, 208, rx, 208, 256)

    def part(k):
        return k * 112

    def mine(at, n):
        return own.at[rows(at, n)]

    tail = pl.ds(448, 16)
    keep = load(own.at[tail], small.at[y])
    tails = [go(own.at[tail], small.at[y], d) for d in (dyu, dyd, dyo)]
    half = (
        go(mine(part(yo), 48), rfh.at[0, pl.ds(0, 48)], dyu),
        go(mine(part(yo) + 48, 64), rfh.at[1], dyd),
    )
    half[0].wait_recv()
    add(own, part(yu), rfh.at[0], 0, 48)
    full_up = go(mine(part(yu), 112), rff.at[0], dyu)
    half[1].wait_recv()
    add(own, part(yd) + 48, rfh.at[1], 0, 64)
    full_down = go(mine(part(yd), 112), rff.at[1], dyd)
    keep.wait()
    for cp in tails:
        cp.wait_recv()
    for cp in tails:
        cp.wait_send()
    total = small[0].astype(jnp.float32)
    for k in range(1, 4):
        total = total + small[k].astype(jnp.float32)
    rx[tail] = total.astype(rx.dtype)
    last = load(rx.at[tail], out.at[tail])
    full_up.wait_recv()
    add(own, part(y), rff.at[0], 0, 112)
    full_down.wait_recv()
    add(own, part(y), rff.at[1], 0, 112)
    here = rows(part(y), 112)
    stay = load(own.at[here], out.at[here])
    up = go(own.at[here], out.at[here], dyu)
    down = go(own.at[here], out.at[here], dyd)
    up.wait_recv()
    lo = rows(part(yd), 48)
    far_up = go(out.at[lo], out.at[lo], dyu)
    down.wait_recv()
    hi = rows(part(yu) + 48, 64)
    far_down = go(out.at[hi], out.at[hi], dyd)
    far_up.wait_recv()
    far_down.wait_recv()
    last.wait()
    stay.wait()
    for cp in go.all:
        if not any(cp is other for other in tails):
            cp.wait_send()


def reduce_grads(gexp, gden, cid=1):
    w = gexp.shape[-1]
    low = jnp.bfloat16
    n = 90
    return pl.pallas_call(
        reduce_kernel,
        out_shape=jax.ShapeDtypeStruct((464, w), low),
        in_specs=[pl.BlockSpec(memory_space=pl.ANY)] * 2,
        out_specs=pl.BlockSpec(memory_space=pl.ANY),
        scratch_shapes=[
            pltpu.VMEM((2, 4, 464, w), low),
            pltpu.VMEM((2, 4, 464, w), low),
            pltpu.VMEM((6, 2, 32, w), low),
            pltpu.VMEM((6, 2, 64, w), low),
            pltpu.VMEM((2, 2, 144, w), low),
            pltpu.VMEM((2, 2, 272, w), low),
            pltpu.VMEM((464, w), low),
            pltpu.VMEM((2, 64, w), low),
            pltpu.VMEM((2, 112, w), low),
            pltpu.VMEM((4, 16, w), low),
            pltpu.SemaphoreType.DMA((n,)),
            pltpu.SemaphoreType.DMA((n,)),
            pltpu.SemaphoreType.DMA((20,)),
        ],
        compiler_params=pltpu.CompilerParams(
            collective_id=cid, has_side_effects=True, vmem_limit_bytes=60 * 1024 * 1024
        ),
    )(gexp, gden)


HEADS = 12
CAPACITY = 72
LANES = 128
SLOT_ROWS = 80
TOKENS = 208
STEPS = 8
EPSILON = 1e-06
LOW = jnp.bfloat16
F32 = jnp.float32
NT = (((1,), (1,)), ((), ()))
TN = (((0,), (0,)), ((), ()))


def mm(a, b, dims=(((1,), (0,)), ((), ()))):
    return lax.dot_general(a, b, dims, preferred_element_type=F32)


def norm_parts(values):
    centre = values - jnp.mean(values, axis=-1, keepdims=True)
    rstd = lax.rsqrt(jnp.mean(centre * centre, axis=-1, keepdims=True) + EPSILON)
    return centre * rstd, rstd


def norm_back(grad, xhat, rstd, gain):
    h = grad * gain
    return rstd * (
        h - jnp.mean(h, axis=-1, keepdims=True) - xhat * jnp.mean(h * xhat, axis=-1, keepdims=True)
    )


def soft_parts(scores):
    expo = jnp.exp(scores - jnp.max(scores, axis=-1, keepdims=True))
    return expo / jnp.sum(expo, axis=-1, keepdims=True)


def route_tables(routes):
    first, second = routes[:, 0:1], routes[:, 1:2]
    lane = lax.broadcasted_iota(jnp.int32, (TOKENS, LANES), 1)
    hot_one = (lane == first).astype(F32)
    hot_two = (lane == second).astype(F32)
    earlier = (
        lax.broadcasted_iota(jnp.int32, (TOKENS, TOKENS), 1)
        < lax.broadcasted_iota(jnp.int32, (TOKENS, TOKENS), 0)
    ).astype(LOW)
    before_one = mm(earlier, hot_one.astype(LOW))
    before_two = mm(earlier, hot_two.astype(LOW)) + jnp.sum(hot_one, axis=0, keepdims=True)
    slot = lax.broadcasted_iota(jnp.int32, (TOKENS, 256), 1)

    def table(hot, before, picked):
        position = jnp.sum(before * hot, axis=1, keepdims=True).astype(jnp.int32)
        kept = (position < CAPACITY) & (picked >= 0)
        ids = jnp.where(kept, picked * SLOT_ROWS + position, 512)
        return (slot == ids).astype(F32).astype(LOW)

    return table(hot_one, before_one, first), table(hot_two, before_two, second), hot_one, hot_two


def score_mask():
    return lax.broadcasted_iota(jnp.int32, (TOKENS, TOKENS), 1) < 197


def unpack_proj(proj_ref, wp):
    for owner in range(16):
        for k in range(3):
            wp[pl.ds(owner * 48 + k * 16, 16), :] = proj_ref[owner, :, pl.ds(k * 768, 768)]


def expert_block(ref, e):
    return ref[:, :, pl.ds(e * 768, 768)].reshape(384, 768)


def slots_of(e):
    return pl.ds(e * SLOT_ROWS, SLOT_ROWS)


def tanh_part(x):
    return jnp.tanh(0.7978845608028654 * (x + 0.044715 * (x * x * x)))


def forward_kernel(
    at, inputs, received, routes, qkv, proj, router, norms, w_in, w_out, *rest
):
    (sent, section_out, c_u, c_nin, c_pro, c_mix, c_res, c_nrm, c_gate, c_slot, c_pre, c_hid, c_result,
     wp, acc, table_one, table_two) = rest[-17:]
    step = pl.program_id(0)

    @pl.when(step == 0)
    def _():
        u_low = jnp.where(at[1] == 0, inputs[0], received[...])
        c_u[0] = u_low
        u = u_low.astype(F32)
        xhat, _ = norm_parts(u)
        nin = (xhat * norms[0:1, :] + norms[2:3, :]).astype(LOW)
        c_nin[0] = nin
        for k in range(3):
            cols = pl.ds(k * 768, 768)
            c_pro[0, :, cols] = mm(nin, qkv[:, :, cols].reshape(768, 768)).astype(LOW)
        mask = score_mask()
        low_half = lax.broadcasted_iota(jnp.int32, (TOKENS, LANES), 1) < 64
        for pair in range(HEADS // 2):
            q = c_pro[0, :, pl.ds(pair * LANES, LANES)]
            k = c_pro[0, :, pl.ds(768 + pair * LANES, LANES)]
            v = c_pro[0, :, pl.ds(1536 + pair * LANES, LANES)]
            outs = []
            for half in range(2):
                qh = jnp.where(low_half if half == 0 else ~low_half, q, jnp.zeros_like(q))
                scores = jnp.where(mask, mm(qh, k, NT) * 0.125, -1e30)
                outs.append(mm(soft_parts(scores).astype(LOW), v))
            c_mix[0, :, pl.ds(pair * LANES, LANES)] = jnp.where(low_half, outs[0], outs[1]).astype(LOW)
        unpack_proj(proj, wp)
        residual = u + mm(c_mix[0], wp[...])
        c_res[0] = residual
        xhat, _ = norm_parts(residual)
        normed = (xhat * norms[1:2, :] + norms[3:4, :]).astype(LOW)
        c_nrm[0] = normed
        logits = mm(normed, router[...])
        lane = lax.broadcasted_iota(jnp.int32, (TOKENS, LANES), 1)
        c_gate[0] = soft_parts(jnp.where(lane < 3, logits, -1e30))
        one, two, _, _ = route_tables(routes[0])
        table_one[...] = one
        table_two[...] = two
        c_slot[0] = mm(one + two, normed, TN).astype(LOW)
        acc[...] = jnp.zeros_like(acc)

    for e in range(3):
        rows = slots_of(e)
        pre = mm(c_slot[0, rows, :], expert_block(w_in, e), NT)
        c_pre[0, rows, :] = pre
        hidden = (0.5 * pre * (1.0 + tanh_part(pre))).astype(LOW)
        c_hid[0, rows, :] = hidden
        acc[rows, :] += mm(hidden, expert_block(w_out, e))

    @pl.when(step == STEPS - 1)
    def _():
        result = acc[...].astype(LOW)
        c_result[0] = result
        lane = lax.broadcasted_iota(jnp.int32, (TOKENS, LANES), 1)
        gates = c_gate[0]
        gate_one = jnp.sum(jnp.where(lane == routes[0, :, 0:1], gates, 0.0), axis=1, keepdims=True)
        gate_two = jnp.sum(jnp.where(lane == routes[0, :, 1:2], gates, 0.0), axis=1, keepdims=True)
        y = c_res[0] + (mm(table_one[...], result) * gate_one + mm(table_two[...], result) * gate_two)
        y = y.astype(LOW)
        sent[...] = y
        section_out[0] = y[:197]


def whole(shape):
    return pl.BlockSpec(shape, lambda j, at: (0,) * len(shape))


def by_micro(shape):
    return pl.BlockSpec((1,) + shape[1:], lambda j, at: (at[0],) + (0,) * (len(shape) - 1))


def chunk(shape):
    return pl.BlockSpec((1, shape[1], 384), lambda j, at: (at[0], 0, j))


def fixed(shape, index):
    return pl.BlockSpec(shape, lambda j, at: index)


WEIGHT_IN = pl.BlockSpec((2, 192, 2304), lambda j, at: (j, 0, 0))
WEIGHT_OUT = pl.BlockSpec((2, 192, 2304), lambda j, at: (j, 1, 0))
QKV = fixed((16, 48, 2304), (0, 8, 0))
PROJ = fixed((16, 16, 2304), (0, 27, 0))
CACHE = [
    ((2, 197, 768), LOW),
    ((2, TOKENS, 768), LOW),
    ((2, TOKENS, 768), LOW),
    ((2, TOKENS, 2304), LOW),
    ((2, TOKENS, 768), LOW),
    ((2, TOKENS, 768), F32),
    ((2, TOKENS, 768), LOW),
    ((2, TOKENS, LANES), F32),
    ((2, 256, 768), LOW),
    ((2, 3 * SLOT_ROWS, 3072), F32),
    ((2, 3 * SLOT_ROWS, 3072), LOW),
    ((2, 256, 768), LOW),
]
BACK = [
    ((2, 197, 768), F32),
    ((2, 256, 768), LOW),
    ((2, 3 * SLOT_ROWS, 3072), LOW),
    ((2, TOKENS, 768), LOW),
    ((2, TOKENS, 2304), LOW),
    ((2, TOKENS, LANES), LOW),
    ((2, 8, 768), F32),
]


def held(shape):
    return chunk(shape) if shape[-1] == 3072 else by_micro(shape)


def call_tick(body, at, operands, specs, kept, kinds, scratch, flops):
    grown = list(operands)
    grown_specs = list(specs)
    aliases = {}
    if kept is not None:
        for n, array in enumerate(kept):
            aliases[1 + len(grown)] = 1 + n
            grown.append(array)
            grown_specs.append(pl.BlockSpec(memory_space=pl.ANY))
    return pl.pallas_call(
        body,
        out_shape=[jax.ShapeDtypeStruct((TOKENS, 768), LOW)]
        + [jax.ShapeDtypeStruct(shape, kind) for shape, kind in kinds],
        grid_spec=pltpu.PrefetchScalarGridSpec(
            num_scalar_prefetch=1,
            grid=(STEPS,),
            in_specs=grown_specs,
            out_specs=[whole((TOKENS, 768))] + [held(shape) for shape, _ in kinds],
            scratch_shapes=scratch,
        ),
        input_output_aliases=aliases,
        compiler_params=pltpu.CompilerParams(vmem_limit_bytes=60 * 1024 * 1024),
        cost_estimate=pl.CostEstimate(flops=flops, bytes_accessed=40_000_000, transcendentals=1_000_000),
    )(at, *grown)


def forward_tick(at, inputs, received, routes, every, router, norms, kept):
    outs = call_tick(
        forward_kernel,
        at,
        [inputs, received, routes, every, every, router, norms, every, every],
        [
            by_micro(inputs.shape), whole((TOKENS, 768)), by_micro(routes.shape), QKV, PROJ,
            whole(router.shape), whole(norms.shape), WEIGHT_IN, WEIGHT_OUT,
        ],
        kept,
        CACHE,
        [
            pltpu.VMEM((768, 768), LOW),
            pltpu.VMEM((256, 768), F32),
            pltpu.VMEM((TOKENS, 256), LOW),
            pltpu.VMEM((TOKENS, 256), LOW),
        ],
        4_000_000_000,
    )
    return outs[0], outs[1:]


def backward_kernel(
    at, cotangent, returned, routes, qkv, proj, router, norms, w_in, w_out,
    c_u, c_pro, c_res, c_gate, c_pre, c_result, *rest
):
    (sent, section_in_grad, b_gres, b_gpre, b_ga, b_gp, b_gl, b_norm,
     wp, acc, table, grad_normed_part) = rest[-12:]
    step = pl.program_id(0)

    def grad_y():
        return jnp.where(at[1] == 1, cotangent[0], returned[...]).astype(F32)

    @pl.when(step == 0)
    def _():
        gy = grad_y()
        one, two, hot_one, hot_two = route_tables(routes[0])
        table[...] = one + two
        gates = c_gate[0]
        gate_one = jnp.sum(gates * hot_one, axis=1, keepdims=True)
        gate_two = jnp.sum(gates * hot_two, axis=1, keepdims=True)
        b_gres[0] = (
            mm(one, (gy * gate_one).astype(LOW), TN) + mm(two, (gy * gate_two).astype(LOW), TN)
        ).astype(LOW)
        result = c_result[0]
        pick_one = jnp.sum(gy * mm(one, result), axis=1, keepdims=True)
        pick_two = jnp.sum(gy * mm(two, result), axis=1, keepdims=True)
        grad_gates = hot_one * pick_one + hot_two * pick_two
        grad_logits = (
            gates * (grad_gates - jnp.sum(grad_gates * gates, axis=1, keepdims=True))
        ).astype(LOW)
        b_gl[0] = grad_logits
        grad_normed_part[...] = mm(grad_logits, router[...], NT)
        acc[...] = jnp.zeros_like(acc)

    for e in range(3):
        rows = slots_of(e)
        grad_hidden = mm(b_gres[0, rows, :], expert_block(w_out, e), NT)
        x = c_pre[0, rows, :]
        t = tanh_part(x)
        slope = 0.5 * (1.0 + t) + 0.5 * x * (1.0 - t * t) * (
            0.7978845608028654 * (1.0 + 3 * 0.044715 * (x * x))
        )
        grad_pre = (slope * grad_hidden).astype(LOW)
        b_gpre[0, rows, :] = grad_pre
        acc[rows, :] += mm(grad_pre, expert_block(w_in, e))

    @pl.when(step == STEPS - 1)
    def _():
        grad_normed = mm(table[...], acc[...].astype(LOW)) + grad_normed_part[...]
        xhat, rstd = norm_parts(c_res[0])
        b_norm[0, 1:2, :] = jnp.sum(grad_normed * xhat, axis=0, keepdims=True)
        b_norm[0, 3:4, :] = jnp.sum(grad_normed, axis=0, keepdims=True)
        b_norm[0, 4:8, :] = jnp.zeros((4, 768), F32)
        grad_residual = grad_y() + norm_back(grad_normed, xhat, rstd, norms[1:2, :])
        ga = grad_residual.astype(LOW)
        b_ga[0] = ga
        unpack_proj(proj, wp)
        grad_mixed = mm(ga, wp[...], NT).astype(LOW)
        mask = score_mask()
        low_half = lax.broadcasted_iota(jnp.int32, (TOKENS, LANES), 1) < 64
        for pair in range(HEADS // 2):
            q = c_pro[0, :, pl.ds(pair * LANES, LANES)]
            k = c_pro[0, :, pl.ds(768 + pair * LANES, LANES)]
            v = c_pro[0, :, pl.ds(1536 + pair * LANES, LANES)]
            gm = grad_mixed[:, pair * LANES:(pair + 1) * LANES]
            gq, gk, gv = [], [], []
            for half in range(2):
                keep = low_half if half == 0 else ~low_half
                qh = jnp.where(keep, q, jnp.zeros_like(q))
                gh = jnp.where(keep, gm, jnp.zeros_like(gm))
                probs = soft_parts(jnp.where(mask, mm(qh, k, NT) * 0.125, -1e30))
                grad_probs = mm(gh, v, NT)
                gs = (
                    probs * (grad_probs - jnp.sum(grad_probs * probs, axis=-1, keepdims=True))
                ).astype(LOW)
                gq.append(mm(gs, k))
                gk.append(mm(gs, q, TN))
                gv.append(mm(probs.astype(LOW), gm, TN))
            b_gp[0, :, pl.ds(pair * LANES, LANES)] = (jnp.where(low_half, gq[0], gq[1]) * 0.125).astype(LOW)
            b_gp[0, :, pl.ds(768 + pair * LANES, LANES)] = (jnp.where(low_half, gk[0], gk[1]) * 0.125).astype(LOW)
            b_gp[0, :, pl.ds(1536 + pair * LANES, LANES)] = jnp.where(low_half, gv[0], gv[1]).astype(LOW)
        grad_nin = jnp.zeros((TOKENS, 768), F32)
        for k in range(3):
            cols = pl.ds(k * 768, 768)
            grad_nin = grad_nin + mm(b_gp[0, :, cols], qkv[:, :, cols].reshape(768, 768), NT)
        xhat, rstd = norm_parts(c_u[0].astype(F32))
        b_norm[0, 0:1, :] = jnp.sum(grad_nin * xhat, axis=0, keepdims=True)
        b_norm[0, 2:3, :] = jnp.sum(grad_nin, axis=0, keepdims=True)
        grad_in = grad_residual + norm_back(grad_nin, xhat, rstd, norms[0:1, :])
        section_in_grad[0] = grad_in[:197]
        sent[...] = grad_in.astype(LOW)


def backward_tick(at, cotangent, returned, routes, every, router, norms, caches, kept):
    _, c_u, _, c_pro, _, c_res, _, c_gate, _, c_pre, _, c_result = caches
    mine = [c_u, c_pro, c_res, c_gate, c_pre, c_result]
    outs = call_tick(
        backward_kernel,
        at,
        [cotangent, returned, routes, every, every, router, norms, every, every] + mine,
        [
            by_micro(cotangent.shape), whole((TOKENS, 768)), by_micro(routes.shape), QKV, PROJ,
            whole(router.shape), whole(norms.shape), WEIGHT_IN, WEIGHT_OUT,
        ]
        + [held(array.shape) for array in mine],
        kept,
        BACK,
        [
            pltpu.VMEM((768, 768), LOW),
            pltpu.VMEM((256, 768), F32),
            pltpu.VMEM((TOKENS, 256), LOW),
            pltpu.VMEM((TOKENS, 768), F32),
        ],
        6_000_000_000,
    )
    return outs[0], outs[1:]


def weight_kernel(c_nin, c_mix, c_nrm, c_slot, c_hid, b_gres, b_gpre, b_ga, b_gp, b_gl, b_norm, gexp, gden):
    step = pl.program_id(0)

    def both(ref, rows=None):
        if rows is None:
            return jnp.concatenate([ref[0], ref[1]], axis=0)
        return jnp.concatenate([ref[0, rows, :], ref[1, rows, :]], axis=0)

    for e in range(3):
        rows = slots_of(e)
        cols = pl.ds(e * 768, 768)
        first = mm(both(b_gpre, rows), both(c_slot, rows), TN).astype(LOW)
        second = mm(both(c_hid, rows), both(b_gres, rows), TN).astype(LOW)
        for owner in range(2):
            gexp[owner, pl.ds(0, 192), cols] = first[owner * 192:(owner + 1) * 192]
            gexp[owner, pl.ds(192, 192), cols] = second[owner * 192:(owner + 1) * 192]

    for k in range(3):
        @pl.when(step == k)
        def _(k=k):
            cols = pl.ds(k * 768, 768)
            grad = mm(both(c_nin), jnp.concatenate([b_gp[0, :, cols], b_gp[1, :, cols]], axis=0), TN).astype(LOW)
            for owner in range(16):
                gden[owner, pl.ds(0, 48), cols] = grad[owner * 48:(owner + 1) * 48]

    @pl.when(step == 3)
    def _():
        grad = mm(both(c_mix), both(b_ga), TN).astype(LOW)
        for owner in range(16):
            for k in range(3):
                at = owner * 48 + k * 16
                gden[owner, pl.ds(48, 16), pl.ds(k * 768, 768)] = grad[at:at + 16]

    @pl.when(step == 4)
    def _():
        router = mm(both(b_gl), both(c_nrm), TN)[:8]
        small = jnp.concatenate([router, b_norm[0] + b_norm[1]], axis=0).astype(LOW)
        for owner in range(16):
            gden[owner, pl.ds(64, 16), pl.ds(0, 768)] = small
            gden[owner, pl.ds(64, 16), pl.ds(768, 1536)] = jnp.zeros((16, 1536), LOW)


def weight_grads(caches, backs):
    _, _, c_nin, _, c_mix, _, c_nrm, _, c_slot, _, c_hid, _ = caches
    _, b_gres, b_gpre, b_ga, b_gp, b_gl, b_norm = backs
    operands = [c_nin, c_mix, c_nrm, c_slot, c_hid, b_gres, b_gpre, b_ga, b_gp, b_gl, b_norm]

    def spec(shape):
        if shape[-1] == 3072:
            return pl.BlockSpec((2, shape[1], 384), lambda j: (0, 0, j))
        return pl.BlockSpec(shape, lambda j: (0, 0, 0))

    return pl.pallas_call(
        weight_kernel,
        out_shape=[
            jax.ShapeDtypeStruct((16, 384, 2304), LOW),
            jax.ShapeDtypeStruct((16, 80, 2304), LOW),
        ],
        grid=(STEPS,),
        in_specs=[spec(array.shape) for array in operands],
        out_specs=[
            pl.BlockSpec((2, 384, 2304), lambda j: (j, 0, 0)),
            pl.BlockSpec((16, 80, 2304), lambda j: (0, 0, 0)),
        ],
        compiler_params=pltpu.CompilerParams(vmem_limit_bytes=60 * 1024 * 1024),
    )(*operands)


def to_section(value, by):
    pairs = [(i, i + by) for i in range(2) if 0 <= i + by < 2]
    return lax.ppermute(value, "section", pairs)


def local(
    inputs, cotangent, routes, norm_gain, norm_offset, w_qkv, w_proj, w_router, experts_in, experts_out
):
    section = lax.axis_index("section")
    small = jnp.concatenate([w_router[0], norm_gain[0].T, norm_offset[0].T], axis=1)
    own = jnp.concatenate(
        [
            experts_in[0].reshape(192, 2304),
            experts_out[0].reshape(192, 2304),
            w_qkv[0],
            w_proj[0].reshape(3, 16, 768).transpose(1, 0, 2).reshape(16, 2304),
            jnp.pad(small.reshape(16, 21), ((0, 0), (0, 2283))),
        ],
        axis=0,
    )
    every = gather(own, 208).reshape(16, 464, 2304)
    small = every[:, 448:, :21].reshape(768, 7)
    router = jnp.pad(small[:, :3], ((0, 0), (0, LANES - 3)))
    norms = jnp.pad(small[:, 3:].T.astype(F32), ((0, 4), (0, 0)))
    pad = ((0, 0), (0, TOKENS - 197), (0, 0))
    inputs = jnp.pad(inputs[:, 0], pad)
    cotangent = jnp.pad(cotangent[:, 0], pad)
    routes = jnp.pad(routes[0, :, 0], ((0, 0), (0, TOKENS - 197), (0, LANES - 2)), constant_values=-1)
    received = jnp.zeros((TOKENS, 768), LOW)
    caches = None
    for tick in range(3):
        at = jnp.stack([jnp.clip(tick - section, 0, 1), section]).astype(jnp.int32)
        sent, caches = forward_tick(at, inputs, received, routes, every, router, norms, caches)
        if tick < 2:
            received = to_section(sent, 1)
    returned = jnp.zeros((TOKENS, 768), LOW)
    backs = None
    for tick in range(3):
        at = jnp.stack([jnp.clip(tick - 1 + section, 0, 1), section]).astype(jnp.int32)
        sent, backs = backward_tick(at, cotangent, returned, routes, every, router, norms, caches, backs)
        if tick < 2:
            returned = to_section(sent, -1)
    gexp, gden = weight_grads(caches, backs)
    total = reduce_grads(gexp.reshape(2, 4, 2, 384, 2304), gden.reshape(2, 4, 2, 80, 2304)).astype(F32)
    mine = lax.dynamic_slice_in_dim(total[448:, :768], lax.axis_index("shard") * 48, 48, axis=1)
    return (
        caches[0][None, :, None],
        backs[0][None, :, None],
        mine[8:10][None],
        mine[10:12][None],
        total[384:432][None],
        total[432:448].reshape(16, 3, 768).transpose(1, 0, 2).reshape(1, 48, 768),
        mine[:3].T[None],
        total[:192].reshape(1, 192, 3, 768),
        total[192:384].reshape(1, 192, 3, 768),
    )


def solution(mesh):
    return jax.shard_map(
        local,
        mesh=mesh,
        in_specs=(
            P(None, ("replica", "shard"), None, None),
            P(None, ("replica", "shard"), None, None),
            P("section", None, ("replica", "shard"), None, None),
            P("section", None, "shard"),
            P("section", None, "shard"),
            P("section", "shard", None),
            P("section", "shard", None),
            P("section", "shard", None),
            P("section", "shard", None, None),
            P("section", "shard", None, None),
        ),
        out_specs=(
            P("section", None, ("replica", "shard"), None, None),
            P("section", None, ("replica", "shard"), None, None),
            P("section", None, "shard"),
            P("section", None, "shard"),
            P("section", "shard", None),
            P("section", "shard", None),
            P("section", "shard", None),
            P("section", "shard", None, None),
            P("section", "shard", None, None),
        ),
        check_vma=False,
    )
```

```python
import jax
import jax.numpy as jnp
from jax import lax
from jax.experimental import pallas as pl
from jax.experimental.pallas import tpu as pltpu
from jax.sharding import PartitionSpec as P

MESH = pl.DeviceIdType.MESH

def place():
    j = lax.axis_index("shard")
    return j // 8, (j // 2) % 4, j % 2, lax.axis_index("replica")

def at_shard(xl, z, c):
    return {"shard": xl * 8 + z * 2 + c}

class Copies:
    def __init__(self, send, recv):
        self.send, self.recv, self.n, self.all = send, recv, 0, []
    def __call__(self, src, dst, dev):
        cp = pltpu.make_async_remote_copy(src_ref=src, dst_ref=dst, send_sem=self.send.at[self.n], recv_sem=self.recv.at[self.n], device_id=dev, device_id_type=MESH)
        self.n += 1
        cp.start()
        self.all.append(cp)
        return cp

def greet(devs):
    b = pltpu.get_barrier_semaphore()
    for d in devs:
        pl.semaphore_signal(b, inc=1, device_id=d, device_id_type=MESH)
    pl.semaphore_wait(b, len(devs))

def halves(n):
    half = n // 32 * 16
    return (half, n - half)


def gather_kernel(p_rows, q_rows, core, own, out, send, recv, loc):
    xl, z, c, y = place()
    ox, zu, zd, zo = 1 - xl, (z + 1) % 4, (z + 3) % 4, (z + 2) % 4
    yu, yd, yo = (y + 1) % 4, (y + 3) % 4, (y + 2) % 4
    dx, du, dd, dc = at_shard(ox, z, c), at_shard(xl, zu, c), at_shard(xl, zd, c), at_shard(xl, z, 1 - c)
    dyu, dyd = {"replica": yu}, {"replica": yd}
    greet([dx, du, dd, dyu, dyd] + ([dc] if core else []))
    go = Copies(send, recv)
    n = q_rows // 4
    def quarter(k):
        return pl.ds(pl.multiple_of(p_rows + k * n, 16), n)
    def lower(k):
        return pl.ds(pl.multiple_of(p_rows + k * n, 16), halves(n)[0])
    def upper(k):
        return pl.ds(pl.multiple_of(p_rows + k * n + halves(n)[0], 16), halves(n)[1])
    def block(a, b, rows):
        return out.at[a, b, c, rows]
    def pass_on(a, b, rows, dev):
        return go(block(a, b, rows), block(a, b, rows), dev)
    cores = []
    def share(a, b, rows):
        if core:
            cores.append(pass_on(a, b, rows, dc))
    local = pltpu.make_async_copy(own, out.at[xl, z, c], loc)
    local.start()
    mine = quarter(y)
    first = pl.ds(0, p_rows)
    plo, pup = pl.ds(0, halves(p_rows)[0]), pl.ds(halves(p_rows)[0], halves(p_rows)[1])
    def from_own(rows, dev):
        return go(own.at[rows], block(xl, z, rows), dev)
    q_up, q_down, q_over = from_own(mine, du), from_own(mine, dd), from_own(mine, dx)
    p_over = from_own(first, dx)
    p_up, p_down = from_own(first, du), from_own(first, dd)
    q_over.wait_recv()
    q_over_up, q_over_down = pass_on(ox, z, mine, du), pass_on(ox, z, mine, dd)
    spread = []
    def over_y(a, b):
        spread.append((a, b, pass_on(a, b, mine, dyu), pass_on(a, b, mine, dyd)))
    q_up.wait_recv()
    f1 = pass_on(xl, zd, lower(y), du)
    over_y(xl, zd)
    q_down.wait_recv()
    f2 = pass_on(xl, zu, upper(y), dd)
    over_y(xl, zu)
    if core:
        cores.append(go(own, out.at[xl, z, c], dc))
    rest_over = [from_own(quarter(k), dx) for k in (yu, yd, yo)]
    q_over_up.wait_recv()
    f3 = pass_on(ox, zd, lower(y), du)
    over_y(ox, zd)
    q_over_down.wait_recv()
    f4 = pass_on(ox, zu, upper(y), dd)
    over_y(ox, zu)
    p_over.wait_recv()
    p_over_up, p_over_down = pass_on(ox, z, first, du), pass_on(ox, z, first, dd)
    f1.wait_recv()
    f2.wait_recv()
    over_y(xl, zo)
    f3.wait_recv()
    f4.wait_recv()
    over_y(ox, zo)
    for a, b in ((xl, zd), (xl, zu), (ox, zd), (ox, zu), (xl, zo), (ox, zo)):
        share(a, b, mine)
    p_up.wait_recv()
    g1 = pass_on(xl, zd, plo, du)
    p_down.wait_recv()
    g2 = pass_on(xl, zu, pup, dd)
    share(xl, zd, first)
    share(xl, zu, first)
    fy = []
    def y_forward(item):
        a, b, up, down = item
        up.wait_recv()
        one = pass_on(a, b, lower(yd), dyu)
        share(a, b, quarter(yd))
        down.wait_recv()
        two = pass_on(a, b, upper(yu), dyd)
        share(a, b, quarter(yu))
        fy.append((a, b, one, two))
    for item in spread[:2]:
        y_forward(item)
    p_over_up.wait_recv()
    g3 = pass_on(ox, zd, plo, du)
    p_over_down.wait_recv()
    g4 = pass_on(ox, zu, pup, dd)
    share(ox, zd, first)
    share(ox, zu, first)
    for item in spread[2:]:
        y_forward(item)
    for cp in rest_over:
        cp.wait_recv()
    share(ox, z, pl.ds(0, p_rows + q_rows))
    for cp in (g1, g2, g3, g4):
        cp.wait_recv()
    share(xl, zo, first)
    share(ox, zo, first)
    for a, b, one, two in fy:
        one.wait_recv()
        two.wait_recv()
        share(a, b, quarter(yo))
    local.wait()
    for cp in cores:
        cp.wait_recv()
    for cp in go.all:
        cp.wait_send()


def gather(own, p_rows, core=True, cid=0):
    r, w = own.shape
    nmax = 80
    def body(own_ref, out_ref, send, recv, loc):
        gather_kernel(p_rows, r - p_rows, core, own_ref, out_ref, send, recv, loc)
    return pl.pallas_call(
        body,
        out_shape=jax.ShapeDtypeStruct((2, 4, 2, r, w), own.dtype),
        in_specs=[pl.BlockSpec(memory_space=pl.ANY)],
        out_specs=pl.BlockSpec(memory_space=pl.ANY),
        scratch_shapes=[pltpu.SemaphoreType.DMA((nmax,)), pltpu.SemaphoreType.DMA((nmax,)), pltpu.SemaphoreType.DMA(())],
        compiler_params=pltpu.CompilerParams(collective_id=cid, has_side_effects=True),
    )(own)


def reduce_kernel(gexp, gden, out, acc, rc, ryh, ryf, rzh, rzf, rx, rfh, rff, tfh, tff, small, send, recv, loc):
    xl, z, c, y = place()
    ox, zu, zd, zo = 1 - xl, (z + 1) % 4, (z + 3) % 4, (z + 2) % 4
    yu, yd, yo = (y + 1) % 4, (y + 3) % 4, (y + 2) % 4
    dx, du, dd, dc = at_shard(ox, z, c), at_shard(xl, zu, c), at_shard(xl, zd, c), at_shard(xl, z, 1 - c)
    dyu, dyd, dyo = {"replica": yu}, {"replica": yd}, {"replica": yo}
    greet([dx, du, dd, dc, dyu, dyd, dyo])
    go = Copies(send, recv)
    locals_ = []

    def load(src, dst):
        cp = pltpu.make_async_copy(src, dst, loc.at[len(locals_)])
        cp.start()
        locals_.append(cp)
        return cp

    def add(dst, dst_at, src, src_at, n):
        def body(i, carry):
            rows = pl.ds(pl.multiple_of(dst_at + i * 16, 16), 16)
            more = pl.ds(pl.multiple_of(src_at + i * 16, 16), 16)
            dst[rows] = dst[rows] + src[more]
            return carry
        lax.fori_loop(0, n // 16, body, 0)

    blocks = [(ox, zo), (xl, zo), (ox, zu), (xl, zu), (ox, zd), (xl, zd), (ox, z), (xl, z)]
    exp_rows, den_rows = pl.ds(80, 384), pl.ds(0, 80)
    parts = []
    for a, b in blocks:
        parts.append((
            load(gexp.at[a, b, c], acc.at[a, b, exp_rows]),
            load(gden.at[a, b, c], acc.at[a, b, den_rows]),
            go(gexp.at[a, b, 1 - c], rc.at[a, b, exp_rows], dc),
            go(gden.at[a, b, 1 - c], rc.at[a, b, den_rows], dc),
        ))

    def own_sum(t):
        a, b = blocks[t]
        one, two, three, four = parts[t]
        one.wait()
        two.wait()
        three.wait_recv()
        four.wait_recv()
        add(acc.at[a, b], 0, rc.at[a, b], 0, 464)

    def quarter(k):
        return 208 + k * 64

    def rows(at, n):
        return pl.ds(pl.multiple_of(at, 16), n)

    def piece(t, at, n):
        a, b = blocks[t]
        return acc.at[a, b, rows(at, n)]

    y_half, y_full, z_half, z_full = {}, {}, {}, {}
    for t in range(6):
        own_sum(t)
        y_half[t] = (
            go(piece(t, quarter(yo), 32), ryh.at[t, 0], dyu),
            go(piece(t, quarter(yo) + 32, 32), ryh.at[t, 1], dyd),
        )
        if t < 2:
            z_half[t, 0] = (
                go(piece(t, 0, 96), rzh.at[t, 0, pl.ds(0, 96)], du),
                go(piece(t, 96, 112), rzh.at[t, 1, pl.ds(0, 112)], dd),
            )
    for t in range(6):
        a, b = blocks[t]
        y_half[t][0].wait_recv()
        add(acc.at[a, b], quarter(yu), ryh.at[t, 0], 0, 32)
        y_full_up = go(piece(t, quarter(yu), 64), ryf.at[t, 0], dyu)
        y_half[t][1].wait_recv()
        add(acc.at[a, b], quarter(yd) + 32, ryh.at[t, 1], 0, 32)
        y_full[t] = (y_full_up, go(piece(t, quarter(yd), 64), ryf.at[t, 1], dyd))
        if t == 1:
            for x in range(2):
                z_half[x, 0][0].wait_recv()
                add(acc.at[blocks[x][0], zu], 0, rzh.at[x, 0], 0, 96)
                up = go(piece(2 + x, 0, 208), rzf.at[x, 0, pl.ds(0, 208)], du)
                z_half[x, 0][1].wait_recv()
                add(acc.at[blocks[x][0], zd], 96, rzh.at[x, 1], 0, 112)
                z_full[x, 0] = (up, go(piece(4 + x, 0, 208), rzf.at[x, 1, pl.ds(0, 208)], dd))
    own_sum(6)
    early = [go(acc.at[ox, z, rows(quarter(k), 64)], rx.at[rows(quarter(k), 64)], dx) for k in (yu, yd, yo)]
    own_sum(7)
    for t in range(6):
        a, b = blocks[t]
        for side in range(2):
            y_full[t][side].wait_recv()
            add(acc.at[a, b], quarter(y), ryf.at[t, side], 0, 64)
        if t < 2:
            z_half[t, 1] = (
                go(piece(t, quarter(y), 32), rzh.at[t, 0, pl.ds(112, 32)], du),
                go(piece(t, quarter(y) + 32, 32), rzh.at[t, 1, pl.ds(112, 32)], dd),
            )
    own = acc.at[xl, z]
    for cp, k in zip(early, (yu, yd, yo)):
        cp.wait_recv()
        add(own, quarter(k), rx, quarter(k), 64)

    def mine(at, n):
        return own.at[rows(at, n)]

    def finish(base, q, halfway, whole_part):
        low, high = halves(q)

        def part(k):
            return base + k * q

        half_up = go(mine(part(yo), low), halfway.at[0, pl.ds(0, low)], dyu)
        half_down = go(mine(part(yo) + low, high), halfway.at[1, pl.ds(0, high)], dyd)
        yield
        half_up.wait_recv()
        add(own, part(yu), halfway.at[0], 0, low)
        full_up = go(mine(part(yu), q), whole_part.at[0], dyu)
        half_down.wait_recv()
        add(own, part(yd) + low, halfway.at[1], 0, high)
        full_down = go(mine(part(yd), q), whole_part.at[1], dyd)
        yield
        full_up.wait_recv()
        add(own, part(y), whole_part.at[0], 0, q)
        full_down.wait_recv()
        add(own, part(y), whole_part.at[1], 0, q)
        here = rows(part(y), q)
        up = go(own.at[here], out.at[here], dyu)
        down = go(own.at[here], out.at[here], dyd)
        stay = load(own.at[here], out.at[here])
        yield
        up.wait_recv()
        lo = rows(part(yd), low)
        far_up = go(out.at[lo], out.at[lo], dyu)
        down.wait_recv()
        hi = rows(part(yu) + low, high)
        far_down = go(out.at[hi], out.at[hi], dyd)
        yield
        far_up.wait_recv()
        far_down.wait_recv()
        stay.wait()
        yield

    over = []
    for x in range(2):
        for side in range(2):
            z_full[x, 0][side].wait_recv()
            add(acc.at[blocks[x][0], z], 0, rzf.at[x, side], 0, 208)
        if x == 0:
            over.append(go(acc.at[ox, z, pl.ds(0, 208)], rx.at[pl.ds(0, 208)], dx))
        z_half[x, 1][0].wait_recv()
        add(acc.at[blocks[x][0], zu], quarter(y), rzh.at[x, 0], 112, 32)
        up = go(piece(2 + x, quarter(y), 64), rzf.at[x, 0, pl.ds(208, 64)], du)
        z_half[x, 1][1].wait_recv()
        add(acc.at[blocks[x][0], zd], quarter(y) + 32, rzh.at[x, 1], 112, 32)
        z_full[x, 1] = (up, go(piece(4 + x, quarter(y), 64), rzf.at[x, 1, pl.ds(208, 64)], dd))
    tail = pl.ds(0, 16)
    end_one = finish(16, 48, tfh, tff)
    end_two = finish(208, 64, rfh, rff)
    for x in range(2):
        for side in range(2):
            z_full[x, 1][side].wait_recv()
            add(acc.at[blocks[x][0], z], quarter(y), rzf.at[x, side], 208, 64)
        if x == 0:
            over.append(go(acc.at[ox, z, rows(quarter(y), 64)], rx.at[rows(quarter(y), 64)], dx))
            over[0].wait_recv()
            add(own, 0, rx, 0, 208)
            keep = load(own.at[tail], small.at[y])
            tails = [go(own.at[tail], small.at[y], d) for d in (dyu, dyd, dyo)]
            next(end_one)
    over[1].wait_recv()
    add(own, quarter(y), rx, quarter(y), 64)
    next(end_two)
    next(end_one)
    next(end_two)
    next(end_one)
    keep.wait()
    for cp in tails:
        cp.wait_recv()
    for cp in tails:
        cp.wait_send()
    total = small[0].astype(jnp.float32)
    for k in range(1, 4):
        total = total + small[k].astype(jnp.float32)
    rx[tail] = total.astype(rx.dtype)
    last = load(rx.at[tail], out.at[tail])
    next(end_two)
    next(end_one)
    next(end_two)
    next(end_one)
    next(end_two)
    last.wait()
    for cp in go.all:
        if not any(cp is other for other in tails):
            cp.wait_send()


def reduce_grads(gexp, gden, cid=1):
    w = gexp.shape[-1]
    low = jnp.bfloat16
    n = 100
    return pl.pallas_call(
        reduce_kernel,
        out_shape=jax.ShapeDtypeStruct((464, w), low),
        in_specs=[pl.BlockSpec(memory_space=pl.ANY)] * 2,
        out_specs=pl.BlockSpec(memory_space=pl.ANY),
        scratch_shapes=[
            pltpu.VMEM((2, 4, 464, w), low),
            pltpu.VMEM((2, 4, 464, w), low),
            pltpu.VMEM((6, 2, 32, w), low),
            pltpu.VMEM((6, 2, 64, w), low),
            pltpu.VMEM((2, 2, 144, w), low),
            pltpu.VMEM((2, 2, 272, w), low),
            pltpu.VMEM((464, w), low),
            pltpu.VMEM((2, 32, w), low),
            pltpu.VMEM((2, 64, w), low),
            pltpu.VMEM((2, 32, w), low),
            pltpu.VMEM((2, 48, w), low),
            pltpu.VMEM((4, 16, w), low),
            pltpu.SemaphoreType.DMA((n,)),
            pltpu.SemaphoreType.DMA((n,)),
            pltpu.SemaphoreType.DMA((20,)),
        ],
        compiler_params=pltpu.CompilerParams(
            collective_id=cid, has_side_effects=True, vmem_limit_bytes=60 * 1024 * 1024
        ),
    )(gexp, gden)


HEADS = 12
CAPACITY = 72
LANES = 128
SLOT_ROWS = 80
TOKENS = 208
STEPS = 4
SPANS = 8
EPSILON = 1e-06
LOW = jnp.bfloat16
F32 = jnp.float32
NT = (((1,), (1,)), ((), ()))
TN = (((0,), (0,)), ((), ()))


def mm(a, b, dims=(((1,), (0,)), ((), ()))):
    return lax.dot_general(a, b, dims, preferred_element_type=F32)


def norm_parts(values):
    centre = values - jnp.mean(values, axis=-1, keepdims=True)
    rstd = lax.rsqrt(jnp.mean(centre * centre, axis=-1, keepdims=True) + EPSILON)
    return centre * rstd, rstd


def norm_back(grad, xhat, rstd, gain):
    h = grad * gain
    return rstd * (
        h - jnp.mean(h, axis=-1, keepdims=True) - xhat * jnp.mean(h * xhat, axis=-1, keepdims=True)
    )


def soft_parts(scores):
    expo = jnp.exp(scores - jnp.max(scores, axis=-1, keepdims=True))
    return expo / jnp.sum(expo, axis=-1, keepdims=True)


def route_tables(routes):
    first, second = routes[:, 0:1], routes[:, 1:2]
    lane = lax.broadcasted_iota(jnp.int32, (TOKENS, LANES), 1)
    hot_one = (lane == first).astype(F32)
    hot_two = (lane == second).astype(F32)
    earlier = (
        lax.broadcasted_iota(jnp.int32, (TOKENS, TOKENS), 1)
        < lax.broadcasted_iota(jnp.int32, (TOKENS, TOKENS), 0)
    ).astype(LOW)
    before_one = mm(earlier, hot_one.astype(LOW))
    before_two = mm(earlier, hot_two.astype(LOW)) + jnp.sum(hot_one, axis=0, keepdims=True)
    slot = lax.broadcasted_iota(jnp.int32, (TOKENS, 256), 1)

    def table(hot, before, picked):
        position = jnp.sum(before * hot, axis=1, keepdims=True).astype(jnp.int32)
        kept = (position < CAPACITY) & (picked >= 0)
        ids = jnp.where(kept, picked * SLOT_ROWS + position, 512)
        return (slot == ids).astype(F32).astype(LOW)

    return table(hot_one, before_one, first), table(hot_two, before_two, second), hot_one, hot_two


def score_mask():
    return lax.broadcasted_iota(jnp.int32, (TOKENS, TOKENS), 1) < 197


def unpack_proj(proj_ref, wp):
    for owner in range(16):
        for k in range(3):
            wp[pl.ds(owner * 48 + k * 16, 16), :] = proj_ref[owner, :, pl.ds(k * 768, 768)]


def slots_of(e):
    return pl.ds(e * SLOT_ROWS, SLOT_ROWS)


def tanh_part(x):
    return jnp.tanh(0.7978845608028654 * (x + 0.044715 * (x * x * x)))


def owners_of(j):
    return pl.ds(j * 4, 4)


def columns_of(j):
    return pl.ds(pl.multiple_of(j * 768, 768), 768)


class Weights:
    def __init__(self, every, experts, qkv, proj, sems):
        self.every, self.experts, self.qkv, self.proj, self.sems = (every, experts, qkv, proj, sems)

    def dense(self):
        return (
            pltpu.make_async_copy(self.every.at[:, pl.ds(384, 48)], self.qkv, self.sems.at[STEPS]),
            pltpu.make_async_copy(self.every.at[:, pl.ds(432, 16)], self.proj, self.sems.at[STEPS + 1]),
        )

    def chunk(self, j):
        return pltpu.make_async_copy(
            self.every.at[owners_of(j), pl.ds(0, 384)], self.experts.at[owners_of(j)], self.sems.at[j]
        )

    def start_dense(self):
        for cp in self.dense():
            cp.start()

    def wait_dense(self):
        for cp in self.dense():
            cp.wait()

    def start_chunks(self):
        for j in range(STEPS):
            self.chunk(j).start()

    def block(self, j, which, e):
        return self.experts[owners_of(j), pl.ds(which * 192, 192), pl.ds(e * 768, 768)].reshape(768, 768)


def weight_scratch():
    return [
        pltpu.VMEM((16, 384, 2304), LOW),
        pltpu.VMEM((16, 48, 2304), LOW),
        pltpu.VMEM((16, 16, 2304), LOW),
        pltpu.SemaphoreType.DMA((STEPS + 2,)),
    ]


def forward_kernel(at, inputs, received, routes, every, router, norms, *rest):
    sent, section_out, *outs = rest[-31:-18]
    (u_at, nin, pro, mix, res, nrm, gate, slot, pre_at, hid, result_at,
     wp, acc, experts, qkv, proj, sems, out_sems) = rest[-18:]
    kept = [u_at, nin, pro, mix, res, nrm, gate, slot, pre_at, hid, result_at]
    micro = at[0]
    weights = Weights(every, experts, qkv, proj, sems)
    weights.start_dense()
    weights.start_chunks()

    def save(n):
        return pltpu.make_async_copy(kept[n], outs[n].at[micro], out_sems.at[n])

    u_low = jnp.where(at[1] == 0, inputs[0], received[...])
    u_at[...] = u_low
    save(0).start()
    u = u_low.astype(F32)
    xhat, _ = norm_parts(u)
    normed_in = (xhat * norms[0:1, :] + norms[2:3, :]).astype(LOW)
    nin[...] = normed_in
    save(1).start()
    one, two, hot_one, hot_two = route_tables(routes[0])
    weights.wait_dense()
    for k in range(3):
        cols = pl.ds(k * 768, 768)
        pro[:, cols] = mm(normed_in, qkv[:, :, cols].reshape(768, 768)).astype(LOW)
    save(2).start()
    mask = score_mask()
    low_half = lax.broadcasted_iota(jnp.int32, (TOKENS, LANES), 1) < 64
    for pair in range(HEADS // 2):
        q = pro[:, pl.ds(pair * LANES, LANES)]
        k = pro[:, pl.ds(768 + pair * LANES, LANES)]
        v = pro[:, pl.ds(1536 + pair * LANES, LANES)]
        sides = []
        for half in range(2):
            qh = jnp.where(low_half if half == 0 else ~low_half, q, jnp.zeros_like(q))
            scores = jnp.where(mask, mm(qh, k, NT) * 0.125, -1e30)
            sides.append(mm(soft_parts(scores).astype(LOW), v))
        mix[:, pl.ds(pair * LANES, LANES)] = jnp.where(low_half, sides[0], sides[1]).astype(LOW)
    save(3).start()
    unpack_proj(proj, wp)
    residual = u + mm(mix[...], wp[...])
    res[...] = residual
    save(4).start()
    xhat, _ = norm_parts(residual)
    normed = (xhat * norms[1:2, :] + norms[3:4, :]).astype(LOW)
    nrm[...] = normed
    save(5).start()
    logits = mm(normed, router[...])
    lane = lax.broadcasted_iota(jnp.int32, (TOKENS, LANES), 1)
    gates = soft_parts(jnp.where(lane < 3, logits, -1e30))
    gate[...] = gates
    save(6).start()
    slot[...] = mm(one + two, normed, TN).astype(LOW)
    save(7).start()
    acc[...] = jnp.zeros_like(acc)

    def step(j, carry):
        weights.chunk(j).wait()
        cols = columns_of(j)
        for e in range(3):
            rows = slots_of(e)
            pre = mm(slot[rows, :], weights.block(j, 0, e), NT)
            pre_at[rows, cols] = pre
            hidden = (0.5 * pre * (1.0 + tanh_part(pre))).astype(LOW)
            hid[rows, cols] = hidden
            acc[rows, :] += mm(hidden, weights.block(j, 1, e))
        return carry

    lax.fori_loop(0, STEPS, step, 0)
    save(8).start()
    save(9).start()
    result = acc[...].astype(LOW)
    result_at[...] = result
    save(10).start()
    gate_one = jnp.sum(gates * hot_one, axis=1, keepdims=True)
    gate_two = jnp.sum(gates * hot_two, axis=1, keepdims=True)
    y = res[...] + (mm(one, result) * gate_one + mm(two, result) * gate_two)
    y = y.astype(LOW)
    sent[...] = y
    section_out[0] = y[:197]
    for n in range(11):
        save(n).wait()


def whole(shape):
    return pl.BlockSpec(shape, lambda j, at: (0,) * len(shape))


def by_micro(shape):
    return pl.BlockSpec((1,) + shape[1:], lambda j, at: (at[0],) + (0,) * (len(shape) - 1))


ANYWHERE = pl.BlockSpec(memory_space=pl.ANY)
CACHE = [
    ((2, 197, 768), LOW),
    ((2, TOKENS, 768), LOW),
    ((2, TOKENS, 768), LOW),
    ((2, TOKENS, 2304), LOW),
    ((2, TOKENS, 768), LOW),
    ((2, TOKENS, 768), F32),
    ((2, TOKENS, 768), LOW),
    ((2, TOKENS, LANES), F32),
    ((2, 256, 768), LOW),
    ((2, 3 * SLOT_ROWS, 3072), F32),
    ((2, 3 * SLOT_ROWS, 3072), LOW),
    ((2, 256, 768), LOW),
]
BACK = [
    ((2, 197, 768), F32),
    ((2, 256, 768), LOW),
    ((2, 3 * SLOT_ROWS, 3072), LOW),
    ((2, TOKENS, 768), LOW),
    ((2, TOKENS, 2304), LOW),
    ((2, TOKENS, LANES), LOW),
    ((2, 8, 768), F32),
]


def call_tick(body, at, operands, specs, kept, kinds, scratch, flops):
    grown = list(operands)
    grown_specs = list(specs)
    aliases = {}
    if kept is not None:
        for n, array in enumerate(kept):
            aliases[1 + len(grown)] = 1 + n
            grown.append(array)
            grown_specs.append(ANYWHERE)
    return pl.pallas_call(
        body,
        out_shape=[jax.ShapeDtypeStruct((TOKENS, 768), LOW)]
        + [jax.ShapeDtypeStruct(shape, kind) for shape, kind in kinds],
        grid_spec=pltpu.PrefetchScalarGridSpec(
            num_scalar_prefetch=1,
            grid=(1,),
            in_specs=grown_specs,
            out_specs=[whole((TOKENS, 768)), by_micro(kinds[0][0])] + [ANYWHERE] * (len(kinds) - 1),
            scratch_shapes=[pltpu.VMEM(shape[1:], kind) for shape, kind in kinds[1:]]
            + scratch
            + weight_scratch()
            + [pltpu.SemaphoreType.DMA((len(kinds),))],
        ),
        input_output_aliases=aliases,
        compiler_params=pltpu.CompilerParams(vmem_limit_bytes=60 * 1024 * 1024),
        cost_estimate=pl.CostEstimate(flops=flops, bytes_accessed=40_000_000, transcendentals=1_000_000),
    )(at, *grown)


def forward_tick(at, inputs, received, routes, every, router, norms, kept):
    outs = call_tick(
        forward_kernel,
        at,
        [inputs, received, routes, every, router, norms],
        [
            by_micro(inputs.shape), whole((TOKENS, 768)), by_micro(routes.shape), ANYWHERE,
            whole(router.shape), whole(norms.shape),
        ],
        kept,
        CACHE,
        [pltpu.VMEM((768, 768), LOW), pltpu.VMEM((256, 768), F32)],
        4_000_000_000,
    )
    return outs[0], outs[1:]


def backward_kernel(
    at, cotangent, returned, routes, every, router, norms, gate, result, h_u, h_pro, h_res, h_pre, *rest
):
    sent, section_in_grad, *outs = rest[-26:-18]
    (gres, gpre, ga_at, gp, gl, gnorm,
     wp, acc, u_at, pro, res, pre_at, in_sems, experts, qkv, proj, sems, out_sems) = rest[-18:]
    kept = [gres, gpre, ga_at, gp, gl, gnorm]
    micro = at[0]
    weights = Weights(every, experts, qkv, proj, sems)
    sources, targets = (h_pre, h_res, h_pro, h_u), (pre_at, res, pro, u_at)

    def fetch(n):
        return pltpu.make_async_copy(sources[n].at[micro], targets[n], in_sems.at[n])

    def save(n):
        return pltpu.make_async_copy(kept[n], outs[n].at[micro], out_sems.at[n])

    fetch(0).start()
    weights.start_chunks()
    weights.start_dense()
    for n in range(1, 4):
        fetch(n).start()
    gy = jnp.where(at[1] == 1, cotangent[0], returned[...]).astype(F32)
    one, two, hot_one, hot_two = route_tables(routes[0])
    gates = gate[0]
    gate_one = jnp.sum(gates * hot_one, axis=1, keepdims=True)
    gate_two = jnp.sum(gates * hot_two, axis=1, keepdims=True)
    gres[...] = (
        mm(one, (gy * gate_one).astype(LOW), TN) + mm(two, (gy * gate_two).astype(LOW), TN)
    ).astype(LOW)
    save(0).start()
    pick_one = jnp.sum(gy * mm(one, result[0]), axis=1, keepdims=True)
    pick_two = jnp.sum(gy * mm(two, result[0]), axis=1, keepdims=True)
    grad_gates = hot_one * pick_one + hot_two * pick_two
    grad_logits = (
        gates * (grad_gates - jnp.sum(grad_gates * gates, axis=1, keepdims=True))
    ).astype(LOW)
    gl[...] = grad_logits
    save(4).start()
    acc[...] = jnp.zeros_like(acc)
    fetch(0).wait()

    def step(j, carry):
        weights.chunk(j).wait()
        cols = columns_of(j)
        for e in range(3):
            rows = slots_of(e)
            grad_hidden = mm(gres[rows, :], weights.block(j, 1, e), NT)
            x = pre_at[rows, cols]
            t = tanh_part(x)
            slope = 0.5 * (1.0 + t) + 0.5 * x * (1.0 - t * t) * (
                0.7978845608028654 * (1.0 + 3 * 0.044715 * (x * x))
            )
            grad_pre = (slope * grad_hidden).astype(LOW)
            gpre[rows, cols] = grad_pre
            acc[rows, :] += mm(grad_pre, weights.block(j, 0, e))
        return carry

    lax.fori_loop(0, STEPS, step, 0)
    save(1).start()
    weights.wait_dense()
    for n in range(1, 4):
        fetch(n).wait()
    grad_normed = mm(one + two, acc[...].astype(LOW)) + mm(grad_logits, router[...], NT)
    xhat, rstd = norm_parts(res[...])
    gnorm[1:2, :] = jnp.sum(grad_normed * xhat, axis=0, keepdims=True)
    gnorm[3:4, :] = jnp.sum(grad_normed, axis=0, keepdims=True)
    gnorm[4:8, :] = jnp.zeros((4, 768), F32)
    grad_residual = gy + norm_back(grad_normed, xhat, rstd, norms[1:2, :])
    ga = grad_residual.astype(LOW)
    ga_at[...] = ga
    save(2).start()
    unpack_proj(proj, wp)
    grad_mixed = mm(ga, wp[...], NT).astype(LOW)
    mask = score_mask()
    low_half = lax.broadcasted_iota(jnp.int32, (TOKENS, LANES), 1) < 64
    for pair in range(HEADS // 2):
        q = pro[:, pl.ds(pair * LANES, LANES)]
        k = pro[:, pl.ds(768 + pair * LANES, LANES)]
        v = pro[:, pl.ds(1536 + pair * LANES, LANES)]
        gm = grad_mixed[:, pair * LANES:(pair + 1) * LANES]
        gq, gk, gv = [], [], []
        for half in range(2):
            keep = low_half if half == 0 else ~low_half
            qh = jnp.where(keep, q, jnp.zeros_like(q))
            gh = jnp.where(keep, gm, jnp.zeros_like(gm))
            probs = soft_parts(jnp.where(mask, mm(qh, k, NT) * 0.125, -1e30))
            grad_probs = mm(gh, v, NT)
            gs = (
                probs * (grad_probs - jnp.sum(grad_probs * probs, axis=-1, keepdims=True))
            ).astype(LOW)
            gq.append(mm(gs, k))
            gk.append(mm(gs, q, TN))
            gv.append(mm(probs.astype(LOW), gm, TN))
        gp[:, pl.ds(pair * LANES, LANES)] = (jnp.where(low_half, gq[0], gq[1]) * 0.125).astype(LOW)
        gp[:, pl.ds(768 + pair * LANES, LANES)] = (jnp.where(low_half, gk[0], gk[1]) * 0.125).astype(LOW)
        gp[:, pl.ds(1536 + pair * LANES, LANES)] = jnp.where(low_half, gv[0], gv[1]).astype(LOW)
    save(3).start()
    grad_nin = jnp.zeros((TOKENS, 768), F32)
    for k in range(3):
        cols = pl.ds(k * 768, 768)
        grad_nin = grad_nin + mm(gp[:, cols], qkv[:, :, cols].reshape(768, 768), NT)
    xhat, rstd = norm_parts(u_at[...].astype(F32))
    gnorm[0:1, :] = jnp.sum(grad_nin * xhat, axis=0, keepdims=True)
    gnorm[2:3, :] = jnp.sum(grad_nin, axis=0, keepdims=True)
    save(5).start()
    grad_in = grad_residual + norm_back(grad_nin, xhat, rstd, norms[0:1, :])
    section_in_grad[0] = grad_in[:197]
    sent[...] = grad_in.astype(LOW)
    for n in range(6):
        save(n).wait()


def backward_tick(at, cotangent, returned, routes, every, router, norms, caches, kept):
    _, c_u, _, c_pro, _, c_res, _, c_gate, _, c_pre, _, c_result = caches
    outs = call_tick(
        backward_kernel,
        at,
        [cotangent, returned, routes, every, router, norms, c_gate, c_result, c_u, c_pro, c_res, c_pre],
        [
            by_micro(cotangent.shape), whole((TOKENS, 768)), by_micro(routes.shape), ANYWHERE,
            whole(router.shape), whole(norms.shape), by_micro(c_gate.shape), by_micro(c_result.shape),
        ]
        + [ANYWHERE] * 4,
        kept,
        BACK,
        [pltpu.VMEM((768, 768), LOW), pltpu.VMEM((256, 768), F32)]
        + [pltpu.VMEM(array.shape[1:], array.dtype) for array in (c_u, c_pro, c_res, c_pre)]
        + [pltpu.SemaphoreType.DMA((4,))],
        6_000_000_000,
    )
    return outs[0], outs[1:]


def weight_kernel(c_nin, c_mix, c_nrm, c_slot, c_hid, b_gres, b_gpre, b_ga, b_gp, b_gl, b_norm, gexp, gden, held_grads, sems):
    step = pl.program_id(0)
    pair = pl.ds(step * 2, 2)

    def both(ref, rows=None):
        if rows is None:
            return jnp.concatenate([ref[0], ref[1]], axis=0)
        return jnp.concatenate([ref[0, rows, :], ref[1, rows, :]], axis=0)

    for e in range(3):
        rows = slots_of(e)
        cols = pl.ds(e * 768, 768)
        first = mm(both(b_gpre, rows), both(c_slot, rows), TN).astype(LOW)
        second = mm(both(c_hid, rows), both(b_gres, rows), TN).astype(LOW)
        for owner in range(2):
            held_grads[step * 2 + owner, pl.ds(0, 192), cols] = first[owner * 192:(owner + 1) * 192]
            held_grads[step * 2 + owner, pl.ds(192, 192), cols] = second[owner * 192:(owner + 1) * 192]
    pltpu.make_async_copy(held_grads.at[pair], gexp.at[pair], sems.at[step]).start()

    for k in range(3):
        @pl.when(step == k)
        def _(k=k):
            cols = pl.ds(k * 768, 768)
            grad = mm(both(c_nin), jnp.concatenate([b_gp[0, :, cols], b_gp[1, :, cols]], axis=0), TN).astype(LOW)
            for owner in range(16):
                gden[owner, pl.ds(32, 48), cols] = grad[owner * 48:(owner + 1) * 48]

    @pl.when(step == 3)
    def _():
        grad = mm(both(c_mix), both(b_ga), TN).astype(LOW)
        for owner in range(16):
            for k in range(3):
                at = owner * 48 + k * 16
                gden[owner, pl.ds(16, 16), pl.ds(k * 768, 768)] = grad[at:at + 16]

    @pl.when(step == 4)
    def _():
        router = mm(both(b_gl), both(c_nrm), TN)[:8]
        small = jnp.concatenate([router, b_norm[0] + b_norm[1]], axis=0).astype(LOW)
        for owner in range(16):
            gden[owner, pl.ds(0, 16), pl.ds(0, 768)] = small
            gden[owner, pl.ds(0, 16), pl.ds(768, 1536)] = jnp.zeros((16, 1536), LOW)

    @pl.when(step == SPANS - 1)
    def _():
        for k in range(SPANS):
            done = pl.ds(k * 2, 2)
            pltpu.make_async_copy(held_grads.at[done], gexp.at[done], sems.at[k]).wait()


def weight_grads(caches, backs):
    _, _, c_nin, _, c_mix, _, c_nrm, _, c_slot, _, c_hid, _ = caches
    _, b_gres, b_gpre, b_ga, b_gp, b_gl, b_norm = backs
    operands = [c_nin, c_mix, c_nrm, c_slot, c_hid, b_gres, b_gpre, b_ga, b_gp, b_gl, b_norm]

    def spec(shape):
        if shape[-1] == 3072:
            return pl.BlockSpec((2, shape[1], 384), lambda j: (0, 0, j))
        return pl.BlockSpec(shape, lambda j: (0, 0, 0))

    return pl.pallas_call(
        weight_kernel,
        out_shape=[
            jax.ShapeDtypeStruct((16, 384, 2304), LOW),
            jax.ShapeDtypeStruct((16, 80, 2304), LOW),
        ],
        grid=(SPANS,),
        in_specs=[spec(array.shape) for array in operands],
        out_specs=[
            pl.BlockSpec(memory_space=pl.ANY),
            pl.BlockSpec((16, 80, 2304), lambda j: (0, 0, 0)),
        ],
        scratch_shapes=[pltpu.VMEM((16, 384, 2304), LOW), pltpu.SemaphoreType.DMA((SPANS,))],
        compiler_params=pltpu.CompilerParams(vmem_limit_bytes=60 * 1024 * 1024),
    )(*operands)


def spread_kernel(total, g_in, g_out, g_qkv, g_proj, small):
    for e in range(3):
        cols = pl.ds(e * 768, 768)
        g_in[0, :, e, :] = total[pl.ds(80, 192), cols].astype(F32)
        g_out[0, :, e, :] = total[pl.ds(272, 192), cols].astype(F32)
        g_proj[0, pl.ds(e * 16, 16), :] = total[pl.ds(16, 16), cols].astype(F32)
    g_qkv[0] = total[pl.ds(32, 48), :].astype(F32)
    small[...] = total[pl.ds(0, 16), pl.ds(0, 768)].astype(F32)


def spread(total):
    shapes = [(1, 192, 3, 768), (1, 192, 3, 768), (1, 48, 2304), (1, 48, 768), (16, 768)]
    return pl.pallas_call(
        spread_kernel,
        out_shape=[jax.ShapeDtypeStruct(shape, F32) for shape in shapes],
        compiler_params=pltpu.CompilerParams(vmem_limit_bytes=60 * 1024 * 1024),
    )(total)


def to_section(value, by):
    pairs = [(i, i + by) for i in range(2) if 0 <= i + by < 2]
    return lax.ppermute(value, "section", pairs)


def local(
    inputs, cotangent, routes, norm_gain, norm_offset, w_qkv, w_proj, w_router, experts_in, experts_out
):
    section = lax.axis_index("section")
    small = jnp.concatenate([w_router[0], norm_gain[0].T, norm_offset[0].T], axis=1)
    own = jnp.concatenate(
        [
            experts_in[0].reshape(192, 2304),
            experts_out[0].reshape(192, 2304),
            w_qkv[0],
            w_proj[0].reshape(3, 16, 768).transpose(1, 0, 2).reshape(16, 2304),
            jnp.pad(small.reshape(16, 21), ((0, 0), (0, 2283))),
        ],
        axis=0,
    )
    every = gather(own, 208).reshape(16, 464, 2304)
    small = every[:, 448:, :21].reshape(768, 7)
    router = jnp.pad(small[:, :3], ((0, 0), (0, LANES - 3)))
    norms = jnp.pad(small[:, 3:].T.astype(F32), ((0, 4), (0, 0)))
    pad = ((0, 0), (0, TOKENS - 197), (0, 0))
    inputs = jnp.pad(inputs[:, 0], pad)
    cotangent = jnp.pad(cotangent[:, 0], pad)
    routes = jnp.pad(routes[0, :, 0], ((0, 0), (0, TOKENS - 197), (0, LANES - 2)), constant_values=-1)
    received = jnp.zeros((TOKENS, 768), LOW)
    caches = None
    for tick in range(3):
        at = jnp.stack([jnp.clip(tick - section, 0, 1), section]).astype(jnp.int32)
        sent, caches = forward_tick(at, inputs, received, routes, every, router, norms, caches)
        if tick < 2:
            received = to_section(sent, 1)
    returned = jnp.zeros((TOKENS, 768), LOW)
    backs = None
    for tick in range(3):
        at = jnp.stack([jnp.clip(tick - 1 + section, 0, 1), section]).astype(jnp.int32)
        sent, backs = backward_tick(at, cotangent, returned, routes, every, router, norms, caches, backs)
        if tick < 2:
            returned = to_section(sent, -1)
    gexp, gden = weight_grads(caches, backs)
    total = reduce_grads(gexp.reshape(2, 4, 2, 384, 2304), gden.reshape(2, 4, 2, 80, 2304))
    g_in, g_out, g_qkv, g_proj, small = spread(total)
    mine = lax.dynamic_slice_in_dim(small, lax.axis_index("shard") * 48, 48, axis=1)
    return (
        caches[0][None, :, None],
        backs[0][None, :, None],
        mine[8:10][None],
        mine[10:12][None],
        g_qkv,
        g_proj,
        mine[:3].T[None],
        g_in,
        g_out,
    )


def solution(mesh):
    return jax.shard_map(
        local,
        mesh=mesh,
        in_specs=(
            P(None, ("replica", "shard"), None, None),
            P(None, ("replica", "shard"), None, None),
            P("section", None, ("replica", "shard"), None, None),
            P("section", None, "shard"),
            P("section", None, "shard"),
            P("section", "shard", None),
            P("section", "shard", None),
            P("section", "shard", None),
            P("section", "shard", None, None),
            P("section", "shard", None, None),
        ),
        out_specs=(
            P("section", None, ("replica", "shard"), None, None),
            P("section", None, ("replica", "shard"), None, None),
            P("section", None, "shard"),
            P("section", None, "shard"),
            P("section", "shard", None),
            P("section", "shard", None),
            P("section", "shard", None),
            P("section", "shard", None, None),
            P("section", "shard", None, None),
        ),
        check_vma=False,
    )
```

```python
import jax
import jax.numpy as jnp
from jax import lax
from jax.experimental import pallas as pl
from jax.experimental.pallas import tpu as pltpu
from jax.sharding import PartitionSpec as P

MESH = pl.DeviceIdType.MESH

def place():
    j = lax.axis_index("shard")
    return j // 8, (j // 2) % 4, j % 2, lax.axis_index("replica")

def at_shard(xl, z, c):
    return {"shard": xl * 8 + z * 2 + c}

class Copies:
    def __init__(self, send, recv):
        self.send, self.recv, self.n, self.all = send, recv, 0, []
    def __call__(self, src, dst, dev):
        cp = pltpu.make_async_remote_copy(src_ref=src, dst_ref=dst, send_sem=self.send.at[self.n], recv_sem=self.recv.at[self.n], device_id=dev, device_id_type=MESH)
        self.n += 1
        cp.start()
        self.all.append(cp)
        return cp

def greet(devs):
    b = pltpu.get_barrier_semaphore()
    for d in devs:
        pl.semaphore_signal(b, inc=1, device_id=d, device_id_type=MESH)
    pl.semaphore_wait(b, len(devs))

def halves(n):
    half = n // 32 * 16
    return (half, n - half)


def gather_kernel(p_rows, q_rows, core, own, out, send, recv, loc):
    xl, z, c, y = place()
    ox, zu, zd, zo = 1 - xl, (z + 1) % 4, (z + 3) % 4, (z + 2) % 4
    yu, yd, yo = (y + 1) % 4, (y + 3) % 4, (y + 2) % 4
    dx, du, dd, dc = at_shard(ox, z, c), at_shard(xl, zu, c), at_shard(xl, zd, c), at_shard(xl, z, 1 - c)
    dyu, dyd = {"replica": yu}, {"replica": yd}
    greet([dx, du, dd, dyu, dyd] + ([dc] if core else []))
    go = Copies(send, recv)
    n = q_rows // 4
    def quarter(k):
        return pl.ds(pl.multiple_of(p_rows + k * n, 16), n)
    def lower(k):
        return pl.ds(pl.multiple_of(p_rows + k * n, 16), halves(n)[0])
    def upper(k):
        return pl.ds(pl.multiple_of(p_rows + k * n + halves(n)[0], 16), halves(n)[1])
    def block(a, b, rows):
        return out.at[a, b, c, rows]
    def pass_on(a, b, rows, dev):
        return go(block(a, b, rows), block(a, b, rows), dev)
    cores = []
    def share(a, b, rows):
        if core:
            cores.append(pass_on(a, b, rows, dc))
    local = pltpu.make_async_copy(own, out.at[xl, z, c], loc)
    local.start()
    mine = quarter(y)
    first, plo, pup = pl.ds(0, 128), pl.ds(0, 64), pl.ds(64, 64)
    cross, clo, cup = pl.ds(128, 80), pl.ds(128, 32), pl.ds(160, 48)
    def from_own(rows, dev):
        return go(own.at[rows], block(xl, z, rows), dev)
    q_up, q_down, q_over = from_own(mine, du), from_own(mine, dd), from_own(mine, dx)
    p_over = from_own(first, dx)
    c_up, c_down, c_over = from_own(cross, du), from_own(cross, dd), from_own(cross, dx)
    p_up, p_down = from_own(first, du), from_own(first, dd)
    q_over.wait_recv()
    q_over_up, q_over_down = pass_on(ox, z, mine, du), pass_on(ox, z, mine, dd)
    spread = []
    def over_y(a, b):
        spread.append((a, b, pass_on(a, b, mine, dyu), pass_on(a, b, mine, dyd)))
    q_up.wait_recv()
    f1 = pass_on(xl, zd, lower(y), du)
    over_y(xl, zd)
    q_down.wait_recv()
    f2 = pass_on(xl, zu, upper(y), dd)
    over_y(xl, zu)
    if core:
        cores.append(go(own, out.at[xl, z, c], dc))
    rest_over = [from_own(quarter(k), dx) for k in (yu, yd, yo)]
    q_over_up.wait_recv()
    f3 = pass_on(ox, zd, lower(y), du)
    over_y(ox, zd)
    q_over_down.wait_recv()
    f4 = pass_on(ox, zu, upper(y), dd)
    over_y(ox, zu)
    c_up.wait_recv()
    h1 = pass_on(xl, zd, clo, du)
    overs = [c_over, pass_on(xl, zd, cross, dx)]
    c_down.wait_recv()
    h2 = pass_on(xl, zu, cup, dd)
    overs.append(pass_on(xl, zu, cross, dx))
    share(xl, zd, cross)
    share(xl, zu, cross)
    p_over.wait_recv()
    p_over_up, p_over_down = pass_on(ox, z, first, du), pass_on(ox, z, first, dd)
    f1.wait_recv()
    f2.wait_recv()
    over_y(xl, zo)
    f3.wait_recv()
    f4.wait_recv()
    over_y(ox, zo)
    h1.wait_recv()
    h2.wait_recv()
    overs.append(pass_on(xl, zo, cross, dx))
    share(xl, zo, cross)
    for a, b in ((xl, zd), (xl, zu), (ox, zd), (ox, zu), (xl, zo), (ox, zo)):
        share(a, b, mine)
    p_up.wait_recv()
    g1 = pass_on(xl, zd, plo, du)
    p_down.wait_recv()
    g2 = pass_on(xl, zu, pup, dd)
    share(xl, zd, first)
    share(xl, zu, first)
    fy = []
    def y_forward(item):
        a, b, up, down = item
        up.wait_recv()
        one = pass_on(a, b, lower(yd), dyu)
        share(a, b, quarter(yd))
        down.wait_recv()
        two = pass_on(a, b, upper(yu), dyd)
        share(a, b, quarter(yu))
        fy.append((a, b, one, two))
    for item in spread[:2]:
        y_forward(item)
    p_over_up.wait_recv()
    g3 = pass_on(ox, zd, plo, du)
    p_over_down.wait_recv()
    g4 = pass_on(ox, zu, pup, dd)
    share(ox, zd, first)
    share(ox, zu, first)
    for item in spread[2:]:
        y_forward(item)
    for cp in rest_over + overs:
        cp.wait_recv()
    share(ox, zd, cross)
    share(ox, zu, cross)
    share(ox, zo, cross)
    share(ox, z, pl.ds(0, p_rows + q_rows))
    for cp in (g1, g2, g3, g4):
        cp.wait_recv()
    share(xl, zo, first)
    share(ox, zo, first)
    for a, b, one, two in fy:
        one.wait_recv()
        two.wait_recv()
        share(a, b, quarter(yo))
    local.wait()
    for cp in cores:
        cp.wait_recv()
    for cp in go.all:
        cp.wait_send()


def gather(own, p_rows, core=True, cid=0):
    r, w = own.shape
    nmax = 110
    def body(own_ref, out_ref, send, recv, loc):
        gather_kernel(p_rows, r - p_rows, core, own_ref, out_ref, send, recv, loc)
    return pl.pallas_call(
        body,
        out_shape=jax.ShapeDtypeStruct((2, 4, 2, r, w), own.dtype),
        in_specs=[pl.BlockSpec(memory_space=pl.ANY)],
        out_specs=pl.BlockSpec(memory_space=pl.ANY),
        scratch_shapes=[pltpu.SemaphoreType.DMA((nmax,)), pltpu.SemaphoreType.DMA((nmax,)), pltpu.SemaphoreType.DMA(())],
        compiler_params=pltpu.CompilerParams(collective_id=cid, has_side_effects=True),
    )(own)


def reduce_kernel(gexp, gden, out, acc, rc, ryh, ryf, rzh, rzf, rx, rfh, rff, tfh, tff, rxx, rch, rcf, small, send, recv, loc):
    xl, z, c, y = place()
    ox, zu, zd, zo = 1 - xl, (z + 1) % 4, (z + 3) % 4, (z + 2) % 4
    yu, yd, yo = (y + 1) % 4, (y + 3) % 4, (y + 2) % 4
    dx, du, dd, dc = at_shard(ox, z, c), at_shard(xl, zu, c), at_shard(xl, zd, c), at_shard(xl, z, 1 - c)
    dyu, dyd, dyo = {"replica": yu}, {"replica": yd}, {"replica": yo}
    greet([dx, du, dd, dc, dyu, dyd, dyo])
    go = Copies(send, recv)
    locals_ = []

    def load(src, dst):
        cp = pltpu.make_async_copy(src, dst, loc.at[len(locals_)])
        cp.start()
        locals_.append(cp)
        return cp

    def add(dst, dst_at, src, src_at, n):
        def body(i, carry):
            rows = pl.ds(pl.multiple_of(dst_at + i * 16, 16), 16)
            more = pl.ds(pl.multiple_of(src_at + i * 16, 16), 16)
            dst[rows] = dst[rows] + src[more]
            return carry
        lax.fori_loop(0, n // 16, body, 0)

    blocks = [(ox, zo), (xl, zo), (ox, zu), (xl, zu), (ox, zd), (xl, zd), (ox, z), (xl, z)]
    exp_rows, den_rows = pl.ds(80, 384), pl.ds(0, 80)
    parts = []
    for a, b in blocks:
        parts.append((
            load(gexp.at[a, b, c], acc.at[a, b, exp_rows]),
            load(gden.at[a, b, c], acc.at[a, b, den_rows]),
            go(gexp.at[a, b, 1 - c], rc.at[a, b, exp_rows], dc),
            go(gden.at[a, b, 1 - c], rc.at[a, b, den_rows], dc),
        ))

    def own_sum(t):
        a, b = blocks[t]
        one, two, three, four = parts[t]
        one.wait()
        two.wait()
        three.wait_recv()
        four.wait_recv()
        add(acc.at[a, b], 0, rc.at[a, b], 0, 464)

    def quarter(k):
        return 208 + k * 64

    def rows(at, n):
        return pl.ds(pl.multiple_of(at, 16), n)

    def piece(t, at, n):
        a, b = blocks[t]
        return acc.at[a, b, rows(at, n)]

    y_half, y_full, z_half, z_full = {}, {}, {}, {}
    cross = []
    for t in range(6):
        own_sum(t)
        y_half[t] = (
            go(piece(t, quarter(yo), 32), ryh.at[t, 0], dyu),
            go(piece(t, quarter(yo) + 32, 32), ryh.at[t, 1], dyd),
        )
        if t < 2:
            z_half[t, 0] = (
                go(piece(t, 0, 64), rzh.at[t, 0, pl.ds(0, 64)], du),
                go(piece(t, 64, 64), rzh.at[t, 1, pl.ds(0, 64)], dd),
            )
        if t % 2 == 0:
            cross.append(go(piece(t, 128, 80), rxx.at[t // 2], dx))
    cross[0].wait_recv()
    add(acc.at[xl, zo], 128, rxx.at[0], 0, 80)
    c_half = (
        go(piece(1, 128, 32), rch.at[0, pl.ds(0, 32)], du),
        go(piece(1, 160, 48), rch.at[1], dd),
    )
    for t in range(6):
        a, b = blocks[t]
        y_half[t][0].wait_recv()
        add(acc.at[a, b], quarter(yu), ryh.at[t, 0], 0, 32)
        y_full_up = go(piece(t, quarter(yu), 64), ryf.at[t, 0], dyu)
        y_half[t][1].wait_recv()
        add(acc.at[a, b], quarter(yd) + 32, ryh.at[t, 1], 0, 32)
        y_full[t] = (y_full_up, go(piece(t, quarter(yd), 64), ryf.at[t, 1], dyd))
        if t == 1:
            for x in range(2):
                z_half[x, 0][0].wait_recv()
                add(acc.at[blocks[x][0], zu], 0, rzh.at[x, 0], 0, 64)
                up = go(piece(2 + x, 0, 128), rzf.at[x, 0, pl.ds(0, 128)], du)
                z_half[x, 0][1].wait_recv()
                add(acc.at[blocks[x][0], zd], 64, rzh.at[x, 1], 0, 64)
                z_full[x, 0] = (up, go(piece(4 + x, 0, 128), rzf.at[x, 1, pl.ds(0, 128)], dd))
        if t == 2:
            own_sum(6)
            early = [
                go(acc.at[ox, z, rows(quarter(k), 64)], rx.at[rows(quarter(k), 64)], dx) for k in (yu, yd, yo)
            ]
            cross.append(go(piece(6, 128, 80), rxx.at[3], dx))
        if t == 3:
            for n, b_at in ((1, zu), (2, zd)):
                cross[n].wait_recv()
                add(acc.at[xl, b_at], 128, rxx.at[n], 0, 80)
            c_half[0].wait_recv()
            add(acc.at[xl, zu], 128, rch.at[0], 0, 32)
            c_full_up = go(piece(3, 128, 80), rcf.at[0], du)
            c_half[1].wait_recv()
            add(acc.at[xl, zd], 160, rch.at[1], 0, 48)
            c_full = (c_full_up, go(piece(5, 128, 80), rcf.at[1], dd))
    own_sum(7)
    for t in range(6):
        a, b = blocks[t]
        for side in range(2):
            y_full[t][side].wait_recv()
            add(acc.at[a, b], quarter(y), ryf.at[t, side], 0, 64)
        if t < 2:
            z_half[t, 1] = (
                go(piece(t, quarter(y), 32), rzh.at[t, 0, pl.ds(112, 32)], du),
                go(piece(t, quarter(y) + 32, 32), rzh.at[t, 1, pl.ds(112, 32)], dd),
            )
    own = acc.at[xl, z]
    for cp, k in zip(early, (yu, yd, yo)):
        cp.wait_recv()
        add(own, quarter(k), rx, quarter(k), 64)

    def mine(at, n):
        return own.at[rows(at, n)]

    def finish(base, q, halfway, whole_part):
        low, high = halves(q)

        def part(k):
            return base + k * q

        half_up = go(mine(part(yo), low), halfway.at[0, pl.ds(0, low)], dyu)
        half_down = go(mine(part(yo) + low, high), halfway.at[1, pl.ds(0, high)], dyd)
        yield
        half_up.wait_recv()
        add(own, part(yu), halfway.at[0], 0, low)
        full_up = go(mine(part(yu), q), whole_part.at[0], dyu)
        half_down.wait_recv()
        add(own, part(yd) + low, halfway.at[1], 0, high)
        full_down = go(mine(part(yd), q), whole_part.at[1], dyd)
        yield
        full_up.wait_recv()
        add(own, part(y), whole_part.at[0], 0, q)
        full_down.wait_recv()
        add(own, part(y), whole_part.at[1], 0, q)
        here = rows(part(y), q)
        up = go(own.at[here], out.at[here], dyu)
        down = go(own.at[here], out.at[here], dyd)
        stay = load(own.at[here], out.at[here])
        yield
        up.wait_recv()
        lo = rows(part(yd), low)
        far_up = go(out.at[lo], out.at[lo], dyu)
        down.wait_recv()
        hi = rows(part(yu) + low, high)
        far_down = go(out.at[hi], out.at[hi], dyd)
        yield
        far_up.wait_recv()
        far_down.wait_recv()
        stay.wait()
        yield

    over = []
    for x in range(2):
        for side in range(2):
            z_full[x, 0][side].wait_recv()
            add(acc.at[blocks[x][0], z], 0, rzf.at[x, side], 0, 128)
        if x == 0:
            over.append(go(acc.at[ox, z, pl.ds(0, 128)], rx.at[pl.ds(0, 128)], dx))
        z_half[x, 1][0].wait_recv()
        add(acc.at[blocks[x][0], zu], quarter(y), rzh.at[x, 0], 112, 32)
        up = go(piece(2 + x, quarter(y), 64), rzf.at[x, 0, pl.ds(208, 64)], du)
        z_half[x, 1][1].wait_recv()
        add(acc.at[blocks[x][0], zd], quarter(y) + 32, rzh.at[x, 1], 112, 32)
        z_full[x, 1] = (up, go(piece(4 + x, quarter(y), 64), rzf.at[x, 1, pl.ds(208, 64)], dd))
    tail = pl.ds(0, 16)
    end_one = finish(16, 48, tfh, tff)
    end_two = finish(208, 64, rfh, rff)
    for x in range(2):
        for side in range(2):
            z_full[x, 1][side].wait_recv()
            add(acc.at[blocks[x][0], z], quarter(y), rzf.at[x, side], 208, 64)
        if x == 0:
            over.append(go(acc.at[ox, z, rows(quarter(y), 64)], rx.at[rows(quarter(y), 64)], dx))
            over[0].wait_recv()
            add(own, 0, rx, 0, 128)
            cross[3].wait_recv()
            add(own, 128, rxx.at[3], 0, 80)
            for side in range(2):
                c_full[side].wait_recv()
                add(own, 128, rcf.at[side], 0, 80)
            keep = load(own.at[tail], small.at[y])
            tails = [go(own.at[tail], small.at[y], d) for d in (dyu, dyd, dyo)]
            next(end_one)
    over[1].wait_recv()
    add(own, quarter(y), rx, quarter(y), 64)
    next(end_two)
    next(end_one)
    next(end_two)
    next(end_one)
    keep.wait()
    for cp in tails:
        cp.wait_recv()
    for cp in tails:
        cp.wait_send()
    total = small[0].astype(jnp.float32)
    for k in range(1, 4):
        total = total + small[k].astype(jnp.float32)
    rx[tail] = total.astype(rx.dtype)
    last = load(rx.at[tail], out.at[tail])
    next(end_two)
    next(end_one)
    next(end_two)
    next(end_one)
    next(end_two)
    last.wait()
    for cp in go.all:
        if not any(cp is other for other in tails):
            cp.wait_send()


def reduce_grads(gexp, gden, cid=1):
    w = gexp.shape[-1]
    low = jnp.bfloat16
    n = 100
    return pl.pallas_call(
        reduce_kernel,
        out_shape=jax.ShapeDtypeStruct((464, w), low),
        in_specs=[pl.BlockSpec(memory_space=pl.ANY)] * 2,
        out_specs=pl.BlockSpec(memory_space=pl.ANY),
        scratch_shapes=[
            pltpu.VMEM((2, 4, 464, w), low),
            pltpu.VMEM((2, 4, 464, w), low),
            pltpu.VMEM((6, 2, 32, w), low),
            pltpu.VMEM((6, 2, 64, w), low),
            pltpu.VMEM((2, 2, 144, w), low),
            pltpu.VMEM((2, 2, 272, w), low),
            pltpu.VMEM((464, w), low),
            pltpu.VMEM((2, 32, w), low),
            pltpu.VMEM((2, 64, w), low),
            pltpu.VMEM((2, 32, w), low),
            pltpu.VMEM((2, 48, w), low),
            pltpu.VMEM((4, 80, w), low),
            pltpu.VMEM((2, 48, w), low),
            pltpu.VMEM((2, 80, w), low),
            pltpu.VMEM((4, 16, w), low),
            pltpu.SemaphoreType.DMA((n,)),
            pltpu.SemaphoreType.DMA((n,)),
            pltpu.SemaphoreType.DMA((20,)),
        ],
        compiler_params=pltpu.CompilerParams(
            collective_id=cid, has_side_effects=True, vmem_limit_bytes=60 * 1024 * 1024
        ),
    )(gexp, gden)


HEADS = 12
CAPACITY = 72
LANES = 128
SLOT_ROWS = 80
TOKENS = 208
STEPS = 4
SPANS = 8
EPSILON = 1e-06
LOW = jnp.bfloat16
F32 = jnp.float32
NT = (((1,), (1,)), ((), ()))
TN = (((0,), (0,)), ((), ()))


def mm(a, b, dims=(((1,), (0,)), ((), ()))):
    return lax.dot_general(a, b, dims, preferred_element_type=F32)


def norm_parts(values):
    centre = values - jnp.mean(values, axis=-1, keepdims=True)
    rstd = lax.rsqrt(jnp.mean(centre * centre, axis=-1, keepdims=True) + EPSILON)
    return centre * rstd, rstd


def norm_back(grad, xhat, rstd, gain):
    h = grad * gain
    return rstd * (
        h - jnp.mean(h, axis=-1, keepdims=True) - xhat * jnp.mean(h * xhat, axis=-1, keepdims=True)
    )


def soft_parts(scores):
    expo = jnp.exp(scores - jnp.max(scores, axis=-1, keepdims=True))
    return expo / jnp.sum(expo, axis=-1, keepdims=True)


def route_tables(routes):
    first, second = routes[:, 0:1], routes[:, 1:2]
    lane = lax.broadcasted_iota(jnp.int32, (TOKENS, LANES), 1)
    hot_one = (lane == first).astype(F32)
    hot_two = (lane == second).astype(F32)
    earlier = (
        lax.broadcasted_iota(jnp.int32, (TOKENS, TOKENS), 1)
        < lax.broadcasted_iota(jnp.int32, (TOKENS, TOKENS), 0)
    ).astype(LOW)
    before_one = mm(earlier, hot_one.astype(LOW))
    before_two = mm(earlier, hot_two.astype(LOW)) + jnp.sum(hot_one, axis=0, keepdims=True)
    slot = lax.broadcasted_iota(jnp.int32, (TOKENS, 256), 1)

    def table(hot, before, picked):
        position = jnp.sum(before * hot, axis=1, keepdims=True).astype(jnp.int32)
        kept = (position < CAPACITY) & (picked >= 0)
        ids = jnp.where(kept, picked * SLOT_ROWS + position, 512)
        return (slot == ids).astype(F32).astype(LOW)

    return table(hot_one, before_one, first), table(hot_two, before_two, second), hot_one, hot_two


def score_mask():
    return lax.broadcasted_iota(jnp.int32, (TOKENS, TOKENS), 1) < 197


def unpack_proj(proj_ref, wp):
    for owner in range(16):
        for k in range(3):
            wp[pl.ds(owner * 48 + k * 16, 16), :] = proj_ref[owner, :, pl.ds(k * 768, 768)]


def slots_of(e):
    return pl.ds(e * SLOT_ROWS, SLOT_ROWS)


def tanh_part(x):
    return jnp.tanh(0.7978845608028654 * (x + 0.044715 * (x * x * x)))


def owners_of(j):
    return pl.ds(j * 4, 4)


def columns_of(j):
    return pl.ds(pl.multiple_of(j * 768, 768), 768)


class Weights:
    def __init__(self, every, experts, qkv, proj, sems):
        self.every, self.experts, self.qkv, self.proj, self.sems = (every, experts, qkv, proj, sems)

    def dense(self):
        return (
            pltpu.make_async_copy(self.every.at[:, pl.ds(384, 48)], self.qkv, self.sems.at[STEPS]),
            pltpu.make_async_copy(self.every.at[:, pl.ds(432, 16)], self.proj, self.sems.at[STEPS + 1]),
        )

    def chunk(self, j):
        return pltpu.make_async_copy(
            self.every.at[owners_of(j), pl.ds(0, 384)], self.experts.at[owners_of(j)], self.sems.at[j]
        )

    def start_dense(self):
        for cp in self.dense():
            cp.start()

    def wait_dense(self):
        for cp in self.dense():
            cp.wait()

    def start_chunks(self):
        for j in range(STEPS):
            self.chunk(j).start()

    def block(self, j, which, e):
        return self.experts[owners_of(j), pl.ds(which * 192, 192), pl.ds(e * 768, 768)].reshape(768, 768)


def weight_scratch():
    return [
        pltpu.VMEM((16, 384, 2304), LOW),
        pltpu.VMEM((16, 48, 2304), LOW),
        pltpu.VMEM((16, 16, 2304), LOW),
        pltpu.SemaphoreType.DMA((STEPS + 2,)),
    ]


def forward_kernel(at, inputs, received, routes, every, router, norms, *rest):
    sent, section_out, *outs = rest[-31:-18]
    (u_at, nin, pro, mix, res, nrm, gate, slot, pre_at, hid, result_at,
     wp, acc, experts, qkv, proj, sems, out_sems) = rest[-18:]
    kept = [u_at, nin, pro, mix, res, nrm, gate, slot, pre_at, hid, result_at]
    micro = at[0]
    weights = Weights(every, experts, qkv, proj, sems)
    weights.start_dense()
    weights.start_chunks()

    def save(n):
        return pltpu.make_async_copy(kept[n], outs[n].at[micro], out_sems.at[n])

    u_low = jnp.where(at[1] == 0, inputs[0], received[...])
    u_at[...] = u_low
    save(0).start()
    u = u_low.astype(F32)
    xhat, _ = norm_parts(u)
    normed_in = (xhat * norms[0:1, :] + norms[2:3, :]).astype(LOW)
    nin[...] = normed_in
    save(1).start()
    one, two, hot_one, hot_two = route_tables(routes[0])
    weights.wait_dense()
    for k in range(3):
        cols = pl.ds(k * 768, 768)
        pro[:, cols] = mm(normed_in, qkv[:, :, cols].reshape(768, 768)).astype(LOW)
    save(2).start()
    mask = score_mask()
    low_half = lax.broadcasted_iota(jnp.int32, (TOKENS, LANES), 1) < 64
    for pair in range(HEADS // 2):
        q = pro[:, pl.ds(pair * LANES, LANES)]
        k = pro[:, pl.ds(768 + pair * LANES, LANES)]
        v = pro[:, pl.ds(1536 + pair * LANES, LANES)]
        sides = []
        for half in range(2):
            qh = jnp.where(low_half if half == 0 else ~low_half, q, jnp.zeros_like(q))
            scores = jnp.where(mask, mm(qh, k, NT) * 0.125, -1e30)
            sides.append(mm(soft_parts(scores).astype(LOW), v))
        mix[:, pl.ds(pair * LANES, LANES)] = jnp.where(low_half, sides[0], sides[1]).astype(LOW)
    save(3).start()
    unpack_proj(proj, wp)
    residual = u + mm(mix[...], wp[...])
    res[...] = residual
    save(4).start()
    xhat, _ = norm_parts(residual)
    normed = (xhat * norms[1:2, :] + norms[3:4, :]).astype(LOW)
    nrm[...] = normed
    save(5).start()
    logits = mm(normed, router[...])
    lane = lax.broadcasted_iota(jnp.int32, (TOKENS, LANES), 1)
    gates = soft_parts(jnp.where(lane < 3, logits, -1e30))
    gate[...] = gates
    save(6).start()
    slot[...] = mm(one + two, normed, TN).astype(LOW)
    save(7).start()
    acc[...] = jnp.zeros_like(acc)

    def step(j, carry):
        weights.chunk(j).wait()
        cols = columns_of(j)
        for e in range(3):
            rows = slots_of(e)
            pre = mm(slot[rows, :], weights.block(j, 0, e), NT)
            pre_at[rows, cols] = pre
            hidden = (0.5 * pre * (1.0 + tanh_part(pre))).astype(LOW)
            hid[rows, cols] = hidden
            acc[rows, :] += mm(hidden, weights.block(j, 1, e))
        return carry

    lax.fori_loop(0, STEPS, step, 0)
    save(8).start()
    save(9).start()
    result = acc[...].astype(LOW)
    result_at[...] = result
    save(10).start()
    gate_one = jnp.sum(gates * hot_one, axis=1, keepdims=True)
    gate_two = jnp.sum(gates * hot_two, axis=1, keepdims=True)
    y = res[...] + (mm(one, result) * gate_one + mm(two, result) * gate_two)
    y = y.astype(LOW)
    sent[...] = y
    section_out[0] = y[:197]
    for n in range(11):
        save(n).wait()


def whole(shape):
    return pl.BlockSpec(shape, lambda j, at: (0,) * len(shape))


def by_micro(shape):
    return pl.BlockSpec((1,) + shape[1:], lambda j, at: (at[0],) + (0,) * (len(shape) - 1))


ANYWHERE = pl.BlockSpec(memory_space=pl.ANY)
CACHE = [
    ((2, 197, 768), LOW),
    ((2, TOKENS, 768), LOW),
    ((2, TOKENS, 768), LOW),
    ((2, TOKENS, 2304), LOW),
    ((2, TOKENS, 768), LOW),
    ((2, TOKENS, 768), F32),
    ((2, TOKENS, 768), LOW),
    ((2, TOKENS, LANES), F32),
    ((2, 256, 768), LOW),
    ((2, 3 * SLOT_ROWS, 3072), F32),
    ((2, 3 * SLOT_ROWS, 3072), LOW),
    ((2, 256, 768), LOW),
]
BACK = [
    ((2, 197, 768), F32),
    ((2, 256, 768), LOW),
    ((2, 3 * SLOT_ROWS, 3072), LOW),
    ((2, TOKENS, 768), LOW),
    ((2, TOKENS, 2304), LOW),
    ((2, TOKENS, LANES), LOW),
    ((2, 8, 768), F32),
]


def call_tick(body, at, operands, specs, kept, kinds, scratch, flops):
    grown = list(operands)
    grown_specs = list(specs)
    aliases = {}
    if kept is not None:
        for n, array in enumerate(kept):
            aliases[1 + len(grown)] = 1 + n
            grown.append(array)
            grown_specs.append(ANYWHERE)
    return pl.pallas_call(
        body,
        out_shape=[jax.ShapeDtypeStruct((TOKENS, 768), LOW)]
        + [jax.ShapeDtypeStruct(shape, kind) for shape, kind in kinds],
        grid_spec=pltpu.PrefetchScalarGridSpec(
            num_scalar_prefetch=1,
            grid=(1,),
            in_specs=grown_specs,
            out_specs=[whole((TOKENS, 768)), by_micro(kinds[0][0])] + [ANYWHERE] * (len(kinds) - 1),
            scratch_shapes=[pltpu.VMEM(shape[1:], kind) for shape, kind in kinds[1:]]
            + scratch
            + weight_scratch()
            + [pltpu.SemaphoreType.DMA((len(kinds),))],
        ),
        input_output_aliases=aliases,
        compiler_params=pltpu.CompilerParams(vmem_limit_bytes=60 * 1024 * 1024),
        cost_estimate=pl.CostEstimate(flops=flops, bytes_accessed=40_000_000, transcendentals=1_000_000),
    )(at, *grown)


def forward_tick(at, inputs, received, routes, every, router, norms, kept):
    outs = call_tick(
        forward_kernel,
        at,
        [inputs, received, routes, every, router, norms],
        [
            by_micro(inputs.shape), whole((TOKENS, 768)), by_micro(routes.shape), ANYWHERE,
            whole(router.shape), whole(norms.shape),
        ],
        kept,
        CACHE,
        [pltpu.VMEM((768, 768), LOW), pltpu.VMEM((256, 768), F32)],
        4_000_000_000,
    )
    return outs[0], outs[1:]


def backward_kernel(
    at, cotangent, returned, routes, every, router, norms, gate, result, h_u, h_pro, h_res, h_pre, *rest
):
    sent, section_in_grad, *outs = rest[-26:-18]
    (gres, gpre, ga_at, gp, gl, gnorm,
     wp, acc, u_at, pro, res, pre_at, in_sems, experts, qkv, proj, sems, out_sems) = rest[-18:]
    kept = [gres, gpre, ga_at, gp, gl, gnorm]
    micro = at[0]
    weights = Weights(every, experts, qkv, proj, sems)
    sources, targets = (h_pre, h_res, h_pro, h_u), (pre_at, res, pro, u_at)

    def fetch(n):
        return pltpu.make_async_copy(sources[n].at[micro], targets[n], in_sems.at[n])

    def save(n):
        return pltpu.make_async_copy(kept[n], outs[n].at[micro], out_sems.at[n])

    fetch(0).start()
    weights.start_chunks()
    weights.start_dense()
    for n in range(1, 4):
        fetch(n).start()
    gy = jnp.where(at[1] == 1, cotangent[0], returned[...]).astype(F32)
    one, two, hot_one, hot_two = route_tables(routes[0])
    gates = gate[0]
    gate_one = jnp.sum(gates * hot_one, axis=1, keepdims=True)
    gate_two = jnp.sum(gates * hot_two, axis=1, keepdims=True)
    gres[...] = (
        mm(one, (gy * gate_one).astype(LOW), TN) + mm(two, (gy * gate_two).astype(LOW), TN)
    ).astype(LOW)
    save(0).start()
    pick_one = jnp.sum(gy * mm(one, result[0]), axis=1, keepdims=True)
    pick_two = jnp.sum(gy * mm(two, result[0]), axis=1, keepdims=True)
    grad_gates = hot_one * pick_one + hot_two * pick_two
    grad_logits = (
        gates * (grad_gates - jnp.sum(grad_gates * gates, axis=1, keepdims=True))
    ).astype(LOW)
    gl[...] = grad_logits
    save(4).start()
    acc[...] = jnp.zeros_like(acc)
    fetch(0).wait()

    def step(j, carry):
        weights.chunk(j).wait()
        cols = columns_of(j)
        for e in range(3):
            rows = slots_of(e)
            grad_hidden = mm(gres[rows, :], weights.block(j, 1, e), NT)
            x = pre_at[rows, cols]
            t = tanh_part(x)
            slope = 0.5 * (1.0 + t) + 0.5 * x * (1.0 - t * t) * (
                0.7978845608028654 * (1.0 + 3 * 0.044715 * (x * x))
            )
            grad_pre = (slope * grad_hidden).astype(LOW)
            gpre[rows, cols] = grad_pre
            acc[rows, :] += mm(grad_pre, weights.block(j, 0, e))
        return carry

    lax.fori_loop(0, STEPS, step, 0)
    save(1).start()
    weights.wait_dense()
    for n in range(1, 4):
        fetch(n).wait()
    grad_normed = mm(one + two, acc[...].astype(LOW)) + mm(grad_logits, router[...], NT)
    xhat, rstd = norm_parts(res[...])
    gnorm[1:2, :] = jnp.sum(grad_normed * xhat, axis=0, keepdims=True)
    gnorm[3:4, :] = jnp.sum(grad_normed, axis=0, keepdims=True)
    gnorm[4:8, :] = jnp.zeros((4, 768), F32)
    grad_residual = gy + norm_back(grad_normed, xhat, rstd, norms[1:2, :])
    ga = grad_residual.astype(LOW)
    ga_at[...] = ga
    save(2).start()
    unpack_proj(proj, wp)
    grad_mixed = mm(ga, wp[...], NT).astype(LOW)
    mask = score_mask()
    low_half = lax.broadcasted_iota(jnp.int32, (TOKENS, LANES), 1) < 64
    for pair in range(HEADS // 2):
        q = pro[:, pl.ds(pair * LANES, LANES)]
        k = pro[:, pl.ds(768 + pair * LANES, LANES)]
        v = pro[:, pl.ds(1536 + pair * LANES, LANES)]
        gm = grad_mixed[:, pair * LANES:(pair + 1) * LANES]
        gq, gk, gv = [], [], []
        for half in range(2):
            keep = low_half if half == 0 else ~low_half
            qh = jnp.where(keep, q, jnp.zeros_like(q))
            gh = jnp.where(keep, gm, jnp.zeros_like(gm))
            probs = soft_parts(jnp.where(mask, mm(qh, k, NT) * 0.125, -1e30))
            grad_probs = mm(gh, v, NT)
            gs = (
                probs * (grad_probs - jnp.sum(grad_probs * probs, axis=-1, keepdims=True))
            ).astype(LOW)
            gq.append(mm(gs, k))
            gk.append(mm(gs, q, TN))
            gv.append(mm(probs.astype(LOW), gm, TN))
        gp[:, pl.ds(pair * LANES, LANES)] = (jnp.where(low_half, gq[0], gq[1]) * 0.125).astype(LOW)
        gp[:, pl.ds(768 + pair * LANES, LANES)] = (jnp.where(low_half, gk[0], gk[1]) * 0.125).astype(LOW)
        gp[:, pl.ds(1536 + pair * LANES, LANES)] = jnp.where(low_half, gv[0], gv[1]).astype(LOW)
    save(3).start()
    grad_nin = jnp.zeros((TOKENS, 768), F32)
    for k in range(3):
        cols = pl.ds(k * 768, 768)
        grad_nin = grad_nin + mm(gp[:, cols], qkv[:, :, cols].reshape(768, 768), NT)
    xhat, rstd = norm_parts(u_at[...].astype(F32))
    gnorm[0:1, :] = jnp.sum(grad_nin * xhat, axis=0, keepdims=True)
    gnorm[2:3, :] = jnp.sum(grad_nin, axis=0, keepdims=True)
    save(5).start()
    grad_in = grad_residual + norm_back(grad_nin, xhat, rstd, norms[0:1, :])
    section_in_grad[0] = grad_in[:197]
    sent[...] = grad_in.astype(LOW)
    for n in range(6):
        save(n).wait()


def backward_tick(at, cotangent, returned, routes, every, router, norms, caches, kept):
    _, c_u, _, c_pro, _, c_res, _, c_gate, _, c_pre, _, c_result = caches
    outs = call_tick(
        backward_kernel,
        at,
        [cotangent, returned, routes, every, router, norms, c_gate, c_result, c_u, c_pro, c_res, c_pre],
        [
            by_micro(cotangent.shape), whole((TOKENS, 768)), by_micro(routes.shape), ANYWHERE,
            whole(router.shape), whole(norms.shape), by_micro(c_gate.shape), by_micro(c_result.shape),
        ]
        + [ANYWHERE] * 4,
        kept,
        BACK,
        [pltpu.VMEM((768, 768), LOW), pltpu.VMEM((256, 768), F32)]
        + [pltpu.VMEM(array.shape[1:], array.dtype) for array in (c_u, c_pro, c_res, c_pre)]
        + [pltpu.SemaphoreType.DMA((4,))],
        6_000_000_000,
    )
    return outs[0], outs[1:]


def weight_kernel(c_nin, c_mix, c_nrm, c_slot, c_hid, b_gres, b_gpre, b_ga, b_gp, b_gl, b_norm, gexp, gden, held_grads, sems):
    step = pl.program_id(0)
    pair = pl.ds(step * 2, 2)

    def both(ref, rows=None):
        if rows is None:
            return jnp.concatenate([ref[0], ref[1]], axis=0)
        return jnp.concatenate([ref[0, rows, :], ref[1, rows, :]], axis=0)

    for e in range(3):
        rows = slots_of(e)
        cols = pl.ds(e * 768, 768)
        first = mm(both(b_gpre, rows), both(c_slot, rows), TN).astype(LOW)
        second = mm(both(c_hid, rows), both(b_gres, rows), TN).astype(LOW)
        for owner in range(2):
            held_grads[step * 2 + owner, pl.ds(0, 192), cols] = first[owner * 192:(owner + 1) * 192]
            held_grads[step * 2 + owner, pl.ds(192, 192), cols] = second[owner * 192:(owner + 1) * 192]
    pltpu.make_async_copy(held_grads.at[pair], gexp.at[pair], sems.at[step]).start()

    for k in range(3):
        @pl.when(step == k)
        def _(k=k):
            cols = pl.ds(k * 768, 768)
            grad = mm(both(c_nin), jnp.concatenate([b_gp[0, :, cols], b_gp[1, :, cols]], axis=0), TN).astype(LOW)
            for owner in range(16):
                gden[owner, pl.ds(32, 48), cols] = grad[owner * 48:(owner + 1) * 48]

    @pl.when(step == 3)
    def _():
        grad = mm(both(c_mix), both(b_ga), TN).astype(LOW)
        for owner in range(16):
            for k in range(3):
                at = owner * 48 + k * 16
                gden[owner, pl.ds(16, 16), pl.ds(k * 768, 768)] = grad[at:at + 16]

    @pl.when(step == 4)
    def _():
        router = mm(both(b_gl), both(c_nrm), TN)[:8]
        small = jnp.concatenate([router, b_norm[0] + b_norm[1]], axis=0).astype(LOW)
        for owner in range(16):
            gden[owner, pl.ds(0, 16), pl.ds(0, 768)] = small
            gden[owner, pl.ds(0, 16), pl.ds(768, 1536)] = jnp.zeros((16, 1536), LOW)

    @pl.when(step == SPANS - 1)
    def _():
        for k in range(SPANS):
            done = pl.ds(k * 2, 2)
            pltpu.make_async_copy(held_grads.at[done], gexp.at[done], sems.at[k]).wait()


def weight_grads(caches, backs):
    _, _, c_nin, _, c_mix, _, c_nrm, _, c_slot, _, c_hid, _ = caches
    _, b_gres, b_gpre, b_ga, b_gp, b_gl, b_norm = backs
    operands = [c_nin, c_mix, c_nrm, c_slot, c_hid, b_gres, b_gpre, b_ga, b_gp, b_gl, b_norm]

    def spec(shape):
        if shape[-1] == 3072:
            return pl.BlockSpec((2, shape[1], 384), lambda j: (0, 0, j))
        return pl.BlockSpec(shape, lambda j: (0, 0, 0))

    return pl.pallas_call(
        weight_kernel,
        out_shape=[
            jax.ShapeDtypeStruct((16, 384, 2304), LOW),
            jax.ShapeDtypeStruct((16, 80, 2304), LOW),
        ],
        grid=(SPANS,),
        in_specs=[spec(array.shape) for array in operands],
        out_specs=[
            pl.BlockSpec(memory_space=pl.ANY),
            pl.BlockSpec((16, 80, 2304), lambda j: (0, 0, 0)),
        ],
        scratch_shapes=[pltpu.VMEM((16, 384, 2304), LOW), pltpu.SemaphoreType.DMA((SPANS,))],
        compiler_params=pltpu.CompilerParams(vmem_limit_bytes=60 * 1024 * 1024),
    )(*operands)


def spread_kernel(total, g_in, g_out, g_qkv, g_proj, small):
    for e in range(3):
        cols = pl.ds(e * 768, 768)
        g_in[0, e] = total[pl.ds(80, 192), cols].astype(F32)
        g_out[0, e] = total[pl.ds(272, 192), cols].astype(F32)
        g_proj[0, pl.ds(e * 16, 16), :] = total[pl.ds(16, 16), cols].astype(F32)
    g_qkv[0] = total[pl.ds(32, 48), :].astype(F32)
    small[...] = total[pl.ds(0, 16), pl.ds(0, 768)].astype(F32)


def spread(total):
    shapes = [(1, 3, 192, 768), (1, 3, 192, 768), (1, 48, 2304), (1, 48, 768), (16, 768)]
    return pl.pallas_call(
        spread_kernel,
        out_shape=[jax.ShapeDtypeStruct(shape, F32) for shape in shapes],
        compiler_params=pltpu.CompilerParams(vmem_limit_bytes=60 * 1024 * 1024),
    )(total)


def hop_kernel(value, out, send, recv):
    peer = {"section": 1 - lax.axis_index("section")}
    greet([peer])
    cp = pltpu.make_async_remote_copy(
        src_ref=value, dst_ref=out, send_sem=send, recv_sem=recv, device_id=peer, device_id_type=MESH
    )
    cp.start()
    cp.wait()


def swap_sections(value):
    return pl.pallas_call(
        hop_kernel,
        out_shape=jax.ShapeDtypeStruct(value.shape, value.dtype),
        in_specs=[pl.BlockSpec(memory_space=pl.ANY)],
        out_specs=pl.BlockSpec(memory_space=pl.ANY),
        scratch_shapes=[pltpu.SemaphoreType.DMA(()), pltpu.SemaphoreType.DMA(())],
        compiler_params=pltpu.CompilerParams(collective_id=2, has_side_effects=True),
    )(value)


def local(
    inputs, cotangent, routes, norm_gain, norm_offset, w_qkv, w_proj, w_router, experts_in, experts_out
):
    section = lax.axis_index("section")
    small = jnp.concatenate([w_router[0], norm_gain[0].T, norm_offset[0].T], axis=1)
    own = jnp.concatenate(
        [
            jnp.concatenate([experts_in[0, :, e] for e in range(3)], axis=1),
            jnp.concatenate([experts_out[0, :, e] for e in range(3)], axis=1),
            w_qkv[0],
            w_proj[0].reshape(3, 16, 768).transpose(1, 0, 2).reshape(16, 2304),
            jnp.pad(small.reshape(16, 21), ((0, 0), (0, 2283))),
        ],
        axis=0,
    )
    every = gather(own, 208).reshape(16, 464, 2304)
    small = every[:, 448:, :21].reshape(768, 7)
    router = jnp.pad(small[:, :3], ((0, 0), (0, LANES - 3)))
    norms = jnp.pad(small[:, 3:].T.astype(F32), ((0, 4), (0, 0)))
    pad = ((0, 0), (0, TOKENS - 197), (0, 0))
    inputs = jnp.pad(inputs[:, 0], pad)
    cotangent = jnp.pad(cotangent[:, 0], pad)
    routes = jnp.pad(routes[0, :, 0], ((0, 0), (0, TOKENS - 197), (0, LANES - 2)), constant_values=-1)
    received = jnp.zeros((TOKENS, 768), LOW)
    caches = None
    for tick in range(3):
        at = jnp.stack([jnp.clip(tick - section, 0, 1), section]).astype(jnp.int32)
        sent, caches = forward_tick(at, inputs, received, routes, every, router, norms, caches)
        if tick < 2:
            received = swap_sections(sent)
    returned = jnp.zeros((TOKENS, 768), LOW)
    backs = None
    for tick in range(3):
        at = jnp.stack([jnp.clip(tick - 1 + section, 0, 1), section]).astype(jnp.int32)
        sent, backs = backward_tick(at, cotangent, returned, routes, every, router, norms, caches, backs)
        if tick < 2:
            returned = swap_sections(sent)
    gexp, gden = weight_grads(caches, backs)
    total = reduce_grads(gexp.reshape(2, 4, 2, 384, 2304), gden.reshape(2, 4, 2, 80, 2304))
    g_in, g_out, g_qkv, g_proj, small = spread(total)
    mine = lax.dynamic_slice_in_dim(small, lax.axis_index("shard") * 48, 48, axis=1)
    return (
        caches[0][None, :, None],
        backs[0][None, :, None],
        mine[8:10][None],
        mine[10:12][None],
        g_qkv,
        g_proj,
        mine[:3].T[None],
        g_in.transpose(0, 2, 1, 3),
        g_out.transpose(0, 2, 1, 3),
    )


def solution(mesh):
    return jax.shard_map(
        local,
        mesh=mesh,
        in_specs=(
            P(None, ("replica", "shard"), None, None),
            P(None, ("replica", "shard"), None, None),
            P("section", None, ("replica", "shard"), None, None),
            P("section", None, "shard"),
            P("section", None, "shard"),
            P("section", "shard", None),
            P("section", "shard", None),
            P("section", "shard", None),
            P("section", "shard", None, None),
            P("section", "shard", None, None),
        ),
        out_specs=(
            P("section", None, ("replica", "shard"), None, None),
            P("section", None, ("replica", "shard"), None, None),
            P("section", None, "shard"),
            P("section", None, "shard"),
            P("section", "shard", None),
            P("section", "shard", None),
            P("section", "shard", None),
            P("section", "shard", None, None),
            P("section", "shard", None, None),
        ),
        check_vma=False,
    )
```

```python
import functools

import jax
import jax.numpy as jnp
from jax import lax
from jax.experimental import pallas as pl
from jax.experimental.pallas import tpu as pltpu
from jax.sharding import PartitionSpec as P

MESH = pl.DeviceIdType.MESH

def place():
    j = lax.axis_index("shard")
    return j // 8, (j // 2) % 4, j % 2, lax.axis_index("replica")

def at_shard(xl, z, c):
    return {"shard": xl * 8 + z * 2 + c}

class Copies:
    def __init__(self, send, recv):
        self.send, self.recv, self.n, self.all = send, recv, 0, []
    def __call__(self, src, dst, dev):
        cp = pltpu.make_async_remote_copy(src_ref=src, dst_ref=dst, send_sem=self.send.at[self.n], recv_sem=self.recv.at[self.n], device_id=dev, device_id_type=MESH)
        self.n += 1
        cp.start()
        self.all.append(cp)
        return cp

def greet(devs):
    b = pltpu.get_barrier_semaphore()
    for d in devs:
        pl.semaphore_signal(b, inc=1, device_id=d, device_id_type=MESH)
    pl.semaphore_wait(b, len(devs))

def halves(n):
    half = n // 32 * 16
    return (half, n - half)


def gather_kernel(p_rows, q_rows, core, own, out, send, recv, loc):
    xl, z, c, y = place()
    ox, zu, zd, zo = 1 - xl, (z + 1) % 4, (z + 3) % 4, (z + 2) % 4
    yu, yd, yo = (y + 1) % 4, (y + 3) % 4, (y + 2) % 4
    dx, du, dd, dc = at_shard(ox, z, c), at_shard(xl, zu, c), at_shard(xl, zd, c), at_shard(xl, z, 1 - c)
    dyu, dyd = {"replica": yu}, {"replica": yd}
    greet([dx, du, dd, dyu, dyd] + ([dc] if core else []))
    go = Copies(send, recv)
    n = q_rows // 4
    def quarter(k):
        return pl.ds(pl.multiple_of(p_rows + k * n, 16), n)
    def lower(k):
        return pl.ds(pl.multiple_of(p_rows + k * n, 16), halves(n)[0])
    def upper(k):
        return pl.ds(pl.multiple_of(p_rows + k * n + halves(n)[0], 16), halves(n)[1])
    def block(a, b, rows):
        return out.at[a, b, c, rows]
    def pass_on(a, b, rows, dev):
        return go(block(a, b, rows), block(a, b, rows), dev)
    cores = []
    def share(a, b, rows):
        if core:
            cores.append(pass_on(a, b, rows, dc))
    local = pltpu.make_async_copy(own, out.at[xl, z, c], loc)
    local.start()
    mine = quarter(y)
    first, plo, pup = pl.ds(0, 128), pl.ds(0, 64), pl.ds(64, 64)
    cross, clo, cup = pl.ds(128, 80), pl.ds(128, 32), pl.ds(160, 48)
    def from_own(rows, dev):
        return go(own.at[rows], block(xl, z, rows), dev)
    q_up, q_down, q_over = from_own(mine, du), from_own(mine, dd), from_own(mine, dx)
    p_over = from_own(first, dx)
    c_up, c_down, c_over = from_own(cross, du), from_own(cross, dd), from_own(cross, dx)
    p_up, p_down = from_own(first, du), from_own(first, dd)
    q_over.wait_recv()
    q_over_up, q_over_down = pass_on(ox, z, mine, du), pass_on(ox, z, mine, dd)
    spread = []
    def over_y(a, b):
        spread.append((a, b, pass_on(a, b, mine, dyu), pass_on(a, b, mine, dyd)))
    q_up.wait_recv()
    f1 = pass_on(xl, zd, lower(y), du)
    over_y(xl, zd)
    q_down.wait_recv()
    f2 = pass_on(xl, zu, upper(y), dd)
    over_y(xl, zu)
    if core:
        cores.append(go(own, out.at[xl, z, c], dc))
    rest_over = [from_own(quarter(k), dx) for k in (yu, yd, yo)]
    q_over_up.wait_recv()
    f3 = pass_on(ox, zd, lower(y), du)
    over_y(ox, zd)
    q_over_down.wait_recv()
    f4 = pass_on(ox, zu, upper(y), dd)
    over_y(ox, zu)
    c_up.wait_recv()
    h1 = pass_on(xl, zd, clo, du)
    overs = [c_over, pass_on(xl, zd, cross, dx)]
    c_down.wait_recv()
    h2 = pass_on(xl, zu, cup, dd)
    overs.append(pass_on(xl, zu, cross, dx))
    share(xl, zd, cross)
    share(xl, zu, cross)
    p_over.wait_recv()
    p_over_up, p_over_down = pass_on(ox, z, first, du), pass_on(ox, z, first, dd)
    f1.wait_recv()
    f2.wait_recv()
    over_y(xl, zo)
    f3.wait_recv()
    f4.wait_recv()
    over_y(ox, zo)
    h1.wait_recv()
    h2.wait_recv()
    overs.append(pass_on(xl, zo, cross, dx))
    share(xl, zo, cross)
    for a, b in ((xl, zd), (xl, zu), (ox, zd), (ox, zu), (xl, zo), (ox, zo)):
        share(a, b, mine)
    p_up.wait_recv()
    g1 = pass_on(xl, zd, plo, du)
    p_down.wait_recv()
    g2 = pass_on(xl, zu, pup, dd)
    share(xl, zd, first)
    share(xl, zu, first)
    fy = []
    def y_forward(item):
        a, b, up, down = item
        up.wait_recv()
        one = pass_on(a, b, lower(yd), dyu)
        share(a, b, quarter(yd))
        down.wait_recv()
        two = pass_on(a, b, upper(yu), dyd)
        share(a, b, quarter(yu))
        fy.append((a, b, one, two))
    for item in spread[:2]:
        y_forward(item)
    p_over_up.wait_recv()
    g3 = pass_on(ox, zd, plo, du)
    p_over_down.wait_recv()
    g4 = pass_on(ox, zu, pup, dd)
    share(ox, zd, first)
    share(ox, zu, first)
    for item in spread[2:]:
        y_forward(item)
    for cp in rest_over + overs:
        cp.wait_recv()
    share(ox, zd, cross)
    share(ox, zu, cross)
    share(ox, zo, cross)
    share(ox, z, pl.ds(0, p_rows + q_rows))
    for cp in (g1, g2, g3, g4):
        cp.wait_recv()
    share(xl, zo, first)
    share(ox, zo, first)
    for a, b, one, two in fy:
        one.wait_recv()
        two.wait_recv()
        share(a, b, quarter(yo))
    local.wait()
    for cp in cores:
        cp.wait_recv()
    for cp in go.all:
        cp.wait_send()


def gather(own, p_rows, core=True, cid=0):
    r, w = own.shape
    nmax = 110
    def body(own_ref, out_ref, send, recv, loc):
        gather_kernel(p_rows, r - p_rows, core, own_ref, out_ref, send, recv, loc)
    return pl.pallas_call(
        body,
        out_shape=jax.ShapeDtypeStruct((2, 4, 2, r, w), own.dtype),
        in_specs=[pl.BlockSpec(memory_space=pl.ANY)],
        out_specs=pl.BlockSpec(memory_space=pl.ANY),
        scratch_shapes=[pltpu.SemaphoreType.DMA((nmax,)), pltpu.SemaphoreType.DMA((nmax,)), pltpu.SemaphoreType.DMA(())],
        compiler_params=pltpu.CompilerParams(collective_id=cid, has_side_effects=True),
    )(own)


def reduce_kernel(gexp, gden, out, acc, rc, ryh, ryf, rzh, rzf, rx, rfh, rff, tfh, tff, rxx, rch, rcf, small, send, recv, loc):
    xl, z, c, y = place()
    ox, zu, zd, zo = 1 - xl, (z + 1) % 4, (z + 3) % 4, (z + 2) % 4
    yu, yd, yo = (y + 1) % 4, (y + 3) % 4, (y + 2) % 4
    dx, du, dd, dc = at_shard(ox, z, c), at_shard(xl, zu, c), at_shard(xl, zd, c), at_shard(xl, z, 1 - c)
    dyu, dyd, dyo = {"replica": yu}, {"replica": yd}, {"replica": yo}
    greet([dx, du, dd, dc, dyu, dyd, dyo])
    go = Copies(send, recv)
    locals_ = []

    def load(src, dst):
        cp = pltpu.make_async_copy(src, dst, loc.at[len(locals_)])
        cp.start()
        locals_.append(cp)
        return cp

    def add(dst, dst_at, src, src_at, n):
        def body(i, carry):
            rows = pl.ds(pl.multiple_of(dst_at + i * 16, 16), 16)
            more = pl.ds(pl.multiple_of(src_at + i * 16, 16), 16)
            dst[rows] = dst[rows] + src[more]
            return carry
        lax.fori_loop(0, n // 16, body, 0)

    blocks = [(ox, zo), (xl, zo), (ox, zu), (xl, zu), (ox, zd), (xl, zd), (ox, z), (xl, z)]
    exp_rows, den_rows = pl.ds(80, 384), pl.ds(0, 80)
    parts = []
    for a, b in blocks:
        parts.append((
            load(gexp.at[a, b, c], acc.at[a, b, exp_rows]),
            load(gden.at[a, b, c], acc.at[a, b, den_rows]),
            go(gexp.at[a, b, 1 - c], rc.at[a, b, exp_rows], dc),
            go(gden.at[a, b, 1 - c], rc.at[a, b, den_rows], dc),
        ))

    def own_sum(t):
        a, b = blocks[t]
        one, two, three, four = parts[t]
        one.wait()
        two.wait()
        three.wait_recv()
        four.wait_recv()
        add(acc.at[a, b], 0, rc.at[a, b], 0, 464)

    def quarter(k):
        return 208 + k * 64

    def rows(at, n):
        return pl.ds(pl.multiple_of(at, 16), n)

    def piece(t, at, n):
        a, b = blocks[t]
        return acc.at[a, b, rows(at, n)]

    y_half, y_full, z_half, z_full = {}, {}, {}, {}
    cross = []
    for t in range(6):
        own_sum(t)
        y_half[t] = (
            go(piece(t, quarter(yo), 32), ryh.at[t, 0], dyu),
            go(piece(t, quarter(yo) + 32, 32), ryh.at[t, 1], dyd),
        )
        if t < 2:
            z_half[t, 0] = (
                go(piece(t, 0, 64), rzh.at[t, 0, pl.ds(0, 64)], du),
                go(piece(t, 64, 64), rzh.at[t, 1, pl.ds(0, 64)], dd),
            )
        if t % 2 == 0:
            cross.append(go(piece(t, 128, 80), rxx.at[t // 2], dx))
    cross[0].wait_recv()
    add(acc.at[xl, zo], 128, rxx.at[0], 0, 80)
    c_half = (
        go(piece(1, 128, 32), rch.at[0, pl.ds(0, 32)], du),
        go(piece(1, 160, 48), rch.at[1], dd),
    )
    for t in range(6):
        a, b = blocks[t]
        y_half[t][0].wait_recv()
        add(acc.at[a, b], quarter(yu), ryh.at[t, 0], 0, 32)
        y_full_up = go(piece(t, quarter(yu), 64), ryf.at[t, 0], dyu)
        y_half[t][1].wait_recv()
        add(acc.at[a, b], quarter(yd) + 32, ryh.at[t, 1], 0, 32)
        y_full[t] = (y_full_up, go(piece(t, quarter(yd), 64), ryf.at[t, 1], dyd))
        if t == 1:
            for x in range(2):
                z_half[x, 0][0].wait_recv()
                add(acc.at[blocks[x][0], zu], 0, rzh.at[x, 0], 0, 64)
                up = go(piece(2 + x, 0, 128), rzf.at[x, 0, pl.ds(0, 128)], du)
                z_half[x, 0][1].wait_recv()
                add(acc.at[blocks[x][0], zd], 64, rzh.at[x, 1], 0, 64)
                z_full[x, 0] = (up, go(piece(4 + x, 0, 128), rzf.at[x, 1, pl.ds(0, 128)], dd))
        if t == 2:
            own_sum(6)
            early = [
                go(acc.at[ox, z, rows(quarter(k), 64)], rx.at[rows(quarter(k), 64)], dx) for k in (yu, yd, yo)
            ]
            cross.append(go(piece(6, 128, 80), rxx.at[3], dx))
        if t == 3:
            for n, b_at in ((1, zu), (2, zd)):
                cross[n].wait_recv()
                add(acc.at[xl, b_at], 128, rxx.at[n], 0, 80)
            c_half[0].wait_recv()
            add(acc.at[xl, zu], 128, rch.at[0], 0, 32)
            c_full_up = go(piece(3, 128, 80), rcf.at[0], du)
            c_half[1].wait_recv()
            add(acc.at[xl, zd], 160, rch.at[1], 0, 48)
            c_full = (c_full_up, go(piece(5, 128, 80), rcf.at[1], dd))
    own_sum(7)
    for t in range(6):
        a, b = blocks[t]
        for side in range(2):
            y_full[t][side].wait_recv()
            add(acc.at[a, b], quarter(y), ryf.at[t, side], 0, 64)
        if t < 2:
            z_half[t, 1] = (
                go(piece(t, quarter(y), 32), rzh.at[t, 0, pl.ds(112, 32)], du),
                go(piece(t, quarter(y) + 32, 32), rzh.at[t, 1, pl.ds(112, 32)], dd),
            )
    own = acc.at[xl, z]
    for cp, k in zip(early, (yu, yd, yo)):
        cp.wait_recv()
        add(own, quarter(k), rx, quarter(k), 64)

    def mine(at, n):
        return own.at[rows(at, n)]

    def finish(base, q, halfway, whole_part):
        low, high = halves(q)

        def part(k):
            return base + k * q

        half_up = go(mine(part(yo), low), halfway.at[0, pl.ds(0, low)], dyu)
        half_down = go(mine(part(yo) + low, high), halfway.at[1, pl.ds(0, high)], dyd)
        yield
        half_up.wait_recv()
        add(own, part(yu), halfway.at[0], 0, low)
        full_up = go(mine(part(yu), q), whole_part.at[0], dyu)
        half_down.wait_recv()
        add(own, part(yd) + low, halfway.at[1], 0, high)
        full_down = go(mine(part(yd), q), whole_part.at[1], dyd)
        yield
        full_up.wait_recv()
        add(own, part(y), whole_part.at[0], 0, q)
        full_down.wait_recv()
        add(own, part(y), whole_part.at[1], 0, q)
        here = rows(part(y), q)
        up = go(own.at[here], out.at[here], dyu)
        down = go(own.at[here], out.at[here], dyd)
        stay = load(own.at[here], out.at[here])
        yield
        up.wait_recv()
        lo = rows(part(yd), low)
        far_up = go(out.at[lo], out.at[lo], dyu)
        down.wait_recv()
        hi = rows(part(yu) + low, high)
        far_down = go(out.at[hi], out.at[hi], dyd)
        yield
        far_up.wait_recv()
        far_down.wait_recv()
        stay.wait()
        yield

    over = []
    for x in range(2):
        for side in range(2):
            z_full[x, 0][side].wait_recv()
            add(acc.at[blocks[x][0], z], 0, rzf.at[x, side], 0, 128)
        if x == 0:
            over.append(go(acc.at[ox, z, pl.ds(0, 128)], rx.at[pl.ds(0, 128)], dx))
        z_half[x, 1][0].wait_recv()
        add(acc.at[blocks[x][0], zu], quarter(y), rzh.at[x, 0], 112, 32)
        up = go(piece(2 + x, quarter(y), 64), rzf.at[x, 0, pl.ds(208, 64)], du)
        z_half[x, 1][1].wait_recv()
        add(acc.at[blocks[x][0], zd], quarter(y) + 32, rzh.at[x, 1], 112, 32)
        z_full[x, 1] = (up, go(piece(4 + x, quarter(y), 64), rzf.at[x, 1, pl.ds(208, 64)], dd))
    tail = pl.ds(0, 16)
    end_one = finish(16, 48, tfh, tff)
    end_two = finish(208, 64, rfh, rff)
    for x in range(2):
        for side in range(2):
            z_full[x, 1][side].wait_recv()
            add(acc.at[blocks[x][0], z], quarter(y), rzf.at[x, side], 208, 64)
        if x == 0:
            over.append(go(acc.at[ox, z, rows(quarter(y), 64)], rx.at[rows(quarter(y), 64)], dx))
            over[0].wait_recv()
            add(own, 0, rx, 0, 128)
            cross[3].wait_recv()
            add(own, 128, rxx.at[3], 0, 80)
            for side in range(2):
                c_full[side].wait_recv()
                add(own, 128, rcf.at[side], 0, 80)
            keep = load(own.at[tail], small.at[y])
            tails = [go(own.at[tail], small.at[y], d) for d in (dyu, dyd, dyo)]
            next(end_one)
    over[1].wait_recv()
    add(own, quarter(y), rx, quarter(y), 64)
    next(end_two)
    next(end_one)
    next(end_two)
    next(end_one)
    keep.wait()
    for cp in tails:
        cp.wait_recv()
    for cp in tails:
        cp.wait_send()
    total = small[0].astype(jnp.float32)
    for k in range(1, 4):
        total = total + small[k].astype(jnp.float32)
    rx[tail] = total.astype(rx.dtype)
    last = load(rx.at[tail], out.at[tail])
    next(end_two)
    next(end_one)
    next(end_two)
    next(end_one)
    next(end_two)
    last.wait()
    for cp in go.all:
        if not any(cp is other for other in tails):
            cp.wait_send()


def reduce_grads(gexp, gden, cid=1):
    w = gexp.shape[-1]
    low = jnp.bfloat16
    n = 100
    return pl.pallas_call(
        reduce_kernel,
        out_shape=jax.ShapeDtypeStruct((464, w), low),
        in_specs=[pl.BlockSpec(memory_space=pl.ANY)] * 2,
        out_specs=pl.BlockSpec(memory_space=pl.ANY),
        scratch_shapes=[
            pltpu.VMEM((2, 4, 464, w), low),
            pltpu.VMEM((2, 4, 464, w), low),
            pltpu.VMEM((6, 2, 32, w), low),
            pltpu.VMEM((6, 2, 64, w), low),
            pltpu.VMEM((2, 2, 144, w), low),
            pltpu.VMEM((2, 2, 272, w), low),
            pltpu.VMEM((464, w), low),
            pltpu.VMEM((2, 32, w), low),
            pltpu.VMEM((2, 64, w), low),
            pltpu.VMEM((2, 32, w), low),
            pltpu.VMEM((2, 48, w), low),
            pltpu.VMEM((4, 80, w), low),
            pltpu.VMEM((2, 48, w), low),
            pltpu.VMEM((2, 80, w), low),
            pltpu.VMEM((4, 16, w), low),
            pltpu.SemaphoreType.DMA((n,)),
            pltpu.SemaphoreType.DMA((n,)),
            pltpu.SemaphoreType.DMA((20,)),
        ],
        compiler_params=pltpu.CompilerParams(
            collective_id=cid, has_side_effects=True, vmem_limit_bytes=60 * 1024 * 1024
        ),
    )(gexp, gden)


HEADS = 12
CAPACITY = 72
LANES = 128
SLOT_ROWS = 80
TOKENS = 208
STEPS = 4
SPANS = 8
EPSILON = 1e-06
LOW = jnp.bfloat16
F32 = jnp.float32
NT = (((1,), (1,)), ((), ()))
TN = (((0,), (0,)), ((), ()))


def mm(a, b, dims=(((1,), (0,)), ((), ()))):
    return lax.dot_general(a, b, dims, preferred_element_type=F32)


def norm_parts(values):
    centre = values - jnp.mean(values, axis=-1, keepdims=True)
    rstd = lax.rsqrt(jnp.mean(centre * centre, axis=-1, keepdims=True) + EPSILON)
    return centre * rstd, rstd


def norm_back(grad, xhat, rstd, gain):
    h = grad * gain
    return rstd * (
        h - jnp.mean(h, axis=-1, keepdims=True) - xhat * jnp.mean(h * xhat, axis=-1, keepdims=True)
    )


def soft_parts(scores):
    expo = jnp.exp(scores - jnp.max(scores, axis=-1, keepdims=True))
    return expo / jnp.sum(expo, axis=-1, keepdims=True)


def route_tables(routes):
    first, second = routes[:, 0:1], routes[:, 1:2]
    lane = lax.broadcasted_iota(jnp.int32, (TOKENS, LANES), 1)
    hot_one = (lane == first).astype(F32)
    hot_two = (lane == second).astype(F32)
    earlier = (
        lax.broadcasted_iota(jnp.int32, (TOKENS, TOKENS), 1)
        < lax.broadcasted_iota(jnp.int32, (TOKENS, TOKENS), 0)
    ).astype(LOW)
    before_one = mm(earlier, hot_one.astype(LOW))
    before_two = mm(earlier, hot_two.astype(LOW)) + jnp.sum(hot_one, axis=0, keepdims=True)
    slot = lax.broadcasted_iota(jnp.int32, (TOKENS, 256), 1)

    def table(hot, before, picked):
        position = jnp.sum(before * hot, axis=1, keepdims=True).astype(jnp.int32)
        kept = (position < CAPACITY) & (picked >= 0)
        ids = jnp.where(kept, picked * SLOT_ROWS + position, 512)
        return (slot == ids).astype(F32).astype(LOW)

    return table(hot_one, before_one, first), table(hot_two, before_two, second), hot_one, hot_two


def score_mask():
    return lax.broadcasted_iota(jnp.int32, (TOKENS, TOKENS), 1) < 197


def unpack_proj(proj_ref, wp):
    for owner in range(16):
        for k in range(3):
            wp[pl.ds(owner * 48 + k * 16, 16), :] = proj_ref[owner, :, pl.ds(k * 768, 768)]


def slots_of(e):
    return pl.ds(e * SLOT_ROWS, SLOT_ROWS)


def tanh_part(x):
    return jnp.tanh(0.7978845608028654 * (x + 0.044715 * (x * x * x)))


def owners_of(j):
    return pl.ds(j * 4, 4)


def columns_of(j):
    return pl.ds(pl.multiple_of(j * 768, 768), 768)


class Weights:
    def __init__(self, every, experts, qkv, proj, sems):
        self.every, self.experts, self.qkv, self.proj, self.sems = (every, experts, qkv, proj, sems)

    def dense(self):
        return (
            pltpu.make_async_copy(self.every.at[:, pl.ds(384, 48)], self.qkv, self.sems.at[STEPS]),
            pltpu.make_async_copy(self.every.at[:, pl.ds(432, 16)], self.proj, self.sems.at[STEPS + 1]),
        )

    def chunk(self, j):
        return pltpu.make_async_copy(
            self.every.at[owners_of(j), pl.ds(0, 384)], self.experts.at[owners_of(j)], self.sems.at[j]
        )

    def start_dense(self):
        for cp in self.dense():
            cp.start()

    def wait_dense(self):
        for cp in self.dense():
            cp.wait()

    def start_chunks(self):
        for j in range(STEPS):
            self.chunk(j).start()

    def block(self, j, which, e):
        return self.experts[owners_of(j), pl.ds(which * 192, 192), pl.ds(e * 768, 768)].reshape(768, 768)


def weight_scratch():
    return [
        pltpu.VMEM((16, 384, 2304), LOW),
        pltpu.VMEM((16, 48, 2304), LOW),
        pltpu.VMEM((16, 16, 2304), LOW),
        pltpu.SemaphoreType.DMA((STEPS + 2,)),
    ]


def forward_kernel(pick, at, inputs, received, routes, every, router, norms, *rest):
    sent, section_out, *outs = rest[-31:-18]
    (u_at, nin, pro, mix, res, nrm, gate, slot, pre_at, hid, result_at,
     wp, acc, experts, qkv, proj, sems, out_sems) = rest[-18:]
    kept = [u_at, nin, pro, mix, res, nrm, gate, slot, pre_at, hid, result_at]
    micro = pick(at)
    weights = Weights(every, experts, qkv, proj, sems)
    weights.start_dense()
    weights.start_chunks()

    def save(n):
        return pltpu.make_async_copy(kept[n], outs[n].at[micro], out_sems.at[n])

    def save_part(n, j):
        cols = columns_of(j)
        return pltpu.make_async_copy(
            kept[n].at[:, cols], outs[n].at[micro, :, cols], out_sems.at[12 + (n - 8) * STEPS + j]
        )

    u_low = jnp.where(at[0] == 0, inputs[0], received[...])
    u_at[...] = u_low
    save(0).start()
    u = u_low.astype(F32)
    xhat, _ = norm_parts(u)
    normed_in = (xhat * norms[0:1, :] + norms[2:3, :]).astype(LOW)
    nin[...] = normed_in
    save(1).start()
    one, two, hot_one, hot_two = route_tables(routes[0])
    weights.wait_dense()
    for k in range(3):
        cols = pl.ds(k * 768, 768)
        pro[:, cols] = mm(normed_in, qkv[:, :, cols].reshape(768, 768)).astype(LOW)
    save(2).start()
    mask = score_mask()
    low_half = lax.broadcasted_iota(jnp.int32, (TOKENS, LANES), 1) < 64
    for pair in range(HEADS // 2):
        q = pro[:, pl.ds(pair * LANES, LANES)]
        k = pro[:, pl.ds(768 + pair * LANES, LANES)]
        v = pro[:, pl.ds(1536 + pair * LANES, LANES)]
        sides = []
        for half in range(2):
            qh = jnp.where(low_half if half == 0 else ~low_half, q, jnp.zeros_like(q))
            scores = jnp.where(mask, mm(qh, k, NT) * 0.125, -1e30)
            sides.append(mm(soft_parts(scores).astype(LOW), v))
        mix[:, pl.ds(pair * LANES, LANES)] = jnp.where(low_half, sides[0], sides[1]).astype(LOW)
    save(3).start()
    unpack_proj(proj, wp)
    residual = u + mm(mix[...], wp[...])
    res[...] = residual
    save(4).start()
    xhat, _ = norm_parts(residual)
    normed = (xhat * norms[1:2, :] + norms[3:4, :]).astype(LOW)
    nrm[...] = normed
    save(5).start()
    logits = mm(normed, router[...])
    lane = lax.broadcasted_iota(jnp.int32, (TOKENS, LANES), 1)
    gates = soft_parts(jnp.where(lane < 3, logits, -1e30))
    gate[...] = gates
    save(6).start()
    slot[...] = mm(one + two, normed, TN).astype(LOW)
    save(7).start()
    acc[...] = jnp.zeros_like(acc)

    def step(j, carry):
        weights.chunk(j).wait()
        cols = columns_of(j)
        for e in range(3):
            rows = slots_of(e)
            pre = mm(slot[rows, :], weights.block(j, 0, e), NT)
            pre_at[rows, cols] = pre.astype(LOW)
            hidden = (0.5 * pre * (1.0 + tanh_part(pre))).astype(LOW)
            hid[rows, cols] = hidden
            acc[rows, :] += mm(hidden, weights.block(j, 1, e))
        save_part(8, j).start()
        save_part(9, j).start()
        return carry

    lax.fori_loop(0, STEPS, step, 0)
    result = acc[...].astype(LOW)
    result_at[...] = result
    save(10).start()
    gate_one = jnp.sum(gates * hot_one, axis=1, keepdims=True)
    gate_two = jnp.sum(gates * hot_two, axis=1, keepdims=True)
    y = res[...] + (mm(one, result) * gate_one + mm(two, result) * gate_two)
    y = y.astype(LOW)
    sent[...] = y
    section_out[0] = y[:197]
    for n in (0, 1, 2, 3, 4, 5, 6, 7, 10):
        save(n).wait()
    for j in range(STEPS):
        save_part(8, j).wait()
        save_part(9, j).wait()


def whole(shape):
    return pl.BlockSpec(shape, lambda j, at: (0,) * len(shape))


def by_micro(shape, pick):
    return pl.BlockSpec((1,) + shape[1:], lambda j, at: (pick(at),) + (0,) * (len(shape) - 1))


ANYWHERE = pl.BlockSpec(memory_space=pl.ANY)
CACHE = [
    ((2, 197, 768), LOW),
    ((2, TOKENS, 768), LOW),
    ((2, TOKENS, 768), LOW),
    ((2, TOKENS, 2304), LOW),
    ((2, TOKENS, 768), LOW),
    ((2, TOKENS, 768), F32),
    ((2, TOKENS, 768), LOW),
    ((2, TOKENS, LANES), F32),
    ((2, 256, 768), LOW),
    ((2, 3 * SLOT_ROWS, 3072), LOW),
    ((2, 3 * SLOT_ROWS, 3072), LOW),
    ((2, 256, 768), LOW),
]
BACK = [
    ((2, 197, 768), F32),
    ((2, 256, 768), LOW),
    ((2, 3 * SLOT_ROWS, 3072), LOW),
    ((2, TOKENS, 768), LOW),
    ((2, TOKENS, 2304), LOW),
    ((2, TOKENS, LANES), LOW),
    ((2, 8, 768), F32),
]


def call_tick(body, pick, at, operands, specs, kept, kinds, scratch, flops):
    grown = list(operands)
    grown_specs = list(specs)
    aliases = {}
    if kept is not None:
        for n, array in enumerate(kept):
            aliases[1 + len(grown)] = 1 + n
            grown.append(array)
            grown_specs.append(ANYWHERE)
    return pl.pallas_call(
        functools.partial(body, pick),
        out_shape=[jax.ShapeDtypeStruct((TOKENS, 768), LOW)]
        + [jax.ShapeDtypeStruct(shape, kind) for shape, kind in kinds],
        grid_spec=pltpu.PrefetchScalarGridSpec(
            num_scalar_prefetch=1,
            grid=(1,),
            in_specs=grown_specs,
            out_specs=[whole((TOKENS, 768)), by_micro(kinds[0][0], pick)] + [ANYWHERE] * (len(kinds) - 1),
            scratch_shapes=[pltpu.VMEM(shape[1:], kind) for shape, kind in kinds[1:]]
            + scratch
            + weight_scratch()
            + [pltpu.SemaphoreType.DMA((len(kinds) + 2 * STEPS,))],
        ),
        input_output_aliases=aliases,
        compiler_params=pltpu.CompilerParams(vmem_limit_bytes=60 * 1024 * 1024),
        cost_estimate=pl.CostEstimate(flops=flops, bytes_accessed=40_000_000, transcendentals=1_000_000),
    )(at, *grown)


def forward_tick(pick, at, inputs, received, routes, every, router, norms, kept):
    outs = call_tick(
        forward_kernel,
        pick,
        at,
        [inputs, received, routes, every, router, norms],
        [
            by_micro(inputs.shape, pick), whole((TOKENS, 768)), by_micro(routes.shape, pick), ANYWHERE,
            whole(router.shape), whole(norms.shape),
        ],
        kept,
        CACHE,
        [pltpu.VMEM((768, 768), LOW), pltpu.VMEM((256, 768), F32)],
        4_000_000_000,
    )
    return outs[0], outs[1:]


def backward_kernel(
    pick, at, cotangent, returned, routes, every, router, norms, gate, result, h_u, h_pro, h_res, h_pre, *rest
):
    sent, section_in_grad, *outs = rest[-26:-18]
    (gres, gpre, ga_at, gp, gl, gnorm,
     wp, acc, u_at, pro, res, pre_at, in_sems, experts, qkv, proj, sems, out_sems) = rest[-18:]
    kept = [gres, gpre, ga_at, gp, gl, gnorm]
    micro = pick(at)
    weights = Weights(every, experts, qkv, proj, sems)
    sources, targets = (h_pre, h_res, h_pro, h_u), (pre_at, res, pro, u_at)

    def fetch(n):
        return pltpu.make_async_copy(sources[n].at[micro], targets[n], in_sems.at[n])

    def save(n):
        return pltpu.make_async_copy(kept[n], outs[n].at[micro], out_sems.at[n])

    fetch(0).start()
    weights.start_chunks()
    weights.start_dense()
    for n in range(1, 4):
        fetch(n).start()
    gy = jnp.where(at[0] == 1, cotangent[0], returned[...]).astype(F32)
    one, two, hot_one, hot_two = route_tables(routes[0])
    gates = gate[0]
    gate_one = jnp.sum(gates * hot_one, axis=1, keepdims=True)
    gate_two = jnp.sum(gates * hot_two, axis=1, keepdims=True)
    gres[...] = (
        mm(one, (gy * gate_one).astype(LOW), TN) + mm(two, (gy * gate_two).astype(LOW), TN)
    ).astype(LOW)
    save(0).start()
    pick_one = jnp.sum(gy * mm(one, result[0]), axis=1, keepdims=True)
    pick_two = jnp.sum(gy * mm(two, result[0]), axis=1, keepdims=True)
    grad_gates = hot_one * pick_one + hot_two * pick_two
    grad_logits = (
        gates * (grad_gates - jnp.sum(grad_gates * gates, axis=1, keepdims=True))
    ).astype(LOW)
    gl[...] = grad_logits
    save(4).start()
    acc[...] = jnp.zeros_like(acc)
    fetch(0).wait()

    def step(j, carry):
        weights.chunk(j).wait()
        cols = columns_of(j)
        for e in range(3):
            rows = slots_of(e)
            grad_hidden = mm(gres[rows, :], weights.block(j, 1, e), NT)
            x = pre_at[rows, cols].astype(F32)
            t = tanh_part(x)
            slope = 0.5 * (1.0 + t) + 0.5 * x * (1.0 - t * t) * (
                0.7978845608028654 * (1.0 + 3 * 0.044715 * (x * x))
            )
            grad_pre = (slope * grad_hidden).astype(LOW)
            gpre[rows, cols] = grad_pre
            acc[rows, :] += mm(grad_pre, weights.block(j, 0, e))
        return carry

    lax.fori_loop(0, STEPS, step, 0)
    save(1).start()
    weights.wait_dense()
    for n in range(1, 4):
        fetch(n).wait()
    grad_normed = mm(one + two, acc[...].astype(LOW)) + mm(grad_logits, router[...], NT)
    xhat, rstd = norm_parts(res[...])
    gnorm[1:2, :] = jnp.sum(grad_normed * xhat, axis=0, keepdims=True)
    gnorm[3:4, :] = jnp.sum(grad_normed, axis=0, keepdims=True)
    gnorm[4:8, :] = jnp.zeros((4, 768), F32)
    grad_residual = gy + norm_back(grad_normed, xhat, rstd, norms[1:2, :])
    ga = grad_residual.astype(LOW)
    ga_at[...] = ga
    save(2).start()
    unpack_proj(proj, wp)
    grad_mixed = mm(ga, wp[...], NT).astype(LOW)
    mask = score_mask()
    low_half = lax.broadcasted_iota(jnp.int32, (TOKENS, LANES), 1) < 64
    for pair in range(HEADS // 2):
        q = pro[:, pl.ds(pair * LANES, LANES)]
        k = pro[:, pl.ds(768 + pair * LANES, LANES)]
        v = pro[:, pl.ds(1536 + pair * LANES, LANES)]
        gm = grad_mixed[:, pair * LANES:(pair + 1) * LANES]
        gq, gk, gv = [], [], []
        for half in range(2):
            keep = low_half if half == 0 else ~low_half
            qh = jnp.where(keep, q, jnp.zeros_like(q))
            gh = jnp.where(keep, gm, jnp.zeros_like(gm))
            probs = soft_parts(jnp.where(mask, mm(qh, k, NT) * 0.125, -1e30))
            grad_probs = mm(gh, v, NT)
            gs = (
                probs * (grad_probs - jnp.sum(grad_probs * probs, axis=-1, keepdims=True))
            ).astype(LOW)
            gq.append(mm(gs, k))
            gk.append(mm(gs, q, TN))
            gv.append(mm(probs.astype(LOW), gm, TN))
        gp[:, pl.ds(pair * LANES, LANES)] = (jnp.where(low_half, gq[0], gq[1]) * 0.125).astype(LOW)
        gp[:, pl.ds(768 + pair * LANES, LANES)] = (jnp.where(low_half, gk[0], gk[1]) * 0.125).astype(LOW)
        gp[:, pl.ds(1536 + pair * LANES, LANES)] = jnp.where(low_half, gv[0], gv[1]).astype(LOW)
    save(3).start()
    grad_nin = jnp.zeros((TOKENS, 768), F32)
    for k in range(3):
        cols = pl.ds(k * 768, 768)
        grad_nin = grad_nin + mm(gp[:, cols], qkv[:, :, cols].reshape(768, 768), NT)
    xhat, rstd = norm_parts(u_at[...].astype(F32))
    gnorm[0:1, :] = jnp.sum(grad_nin * xhat, axis=0, keepdims=True)
    gnorm[2:3, :] = jnp.sum(grad_nin, axis=0, keepdims=True)
    save(5).start()
    grad_in = grad_residual + norm_back(grad_nin, xhat, rstd, norms[0:1, :])
    section_in_grad[0] = grad_in[:197]
    sent[...] = grad_in.astype(LOW)
    for n in range(6):
        save(n).wait()


def backward_tick(pick, at, cotangent, returned, routes, every, router, norms, caches, kept):
    _, c_u, _, c_pro, _, c_res, _, c_gate, _, c_pre, _, c_result = caches
    outs = call_tick(
        backward_kernel,
        pick,
        at,
        [cotangent, returned, routes, every, router, norms, c_gate, c_result, c_u, c_pro, c_res, c_pre],
        [
            by_micro(cotangent.shape, pick), whole((TOKENS, 768)), by_micro(routes.shape, pick), ANYWHERE,
            whole(router.shape), whole(norms.shape), by_micro(c_gate.shape, pick), by_micro(c_result.shape, pick),
        ]
        + [ANYWHERE] * 4,
        kept,
        BACK,
        [pltpu.VMEM((768, 768), LOW), pltpu.VMEM((256, 768), F32)]
        + [pltpu.VMEM(array.shape[1:], array.dtype) for array in (c_u, c_pro, c_res, c_pre)]
        + [pltpu.SemaphoreType.DMA((4,))],
        6_000_000_000,
    )
    return outs[0], outs[1:]


def weight_kernel(c_nin, c_mix, c_nrm, c_slot, c_hid, b_gres, b_gpre, b_ga, b_gp, b_gl, b_norm, gexp, gden, held_grads, sems):
    step = pl.program_id(0)
    pair = pl.ds(step * 2, 2)

    def both(ref, rows=None):
        if rows is None:
            return jnp.concatenate([ref[0], ref[1]], axis=0)
        return jnp.concatenate([ref[0, rows, :], ref[1, rows, :]], axis=0)

    for e in range(3):
        rows = slots_of(e)
        cols = pl.ds(e * 768, 768)
        first = mm(both(b_gpre, rows), both(c_slot, rows), TN).astype(LOW)
        second = mm(both(c_hid, rows), both(b_gres, rows), TN).astype(LOW)
        for owner in range(2):
            held_grads[step * 2 + owner, pl.ds(0, 192), cols] = first[owner * 192:(owner + 1) * 192]
            held_grads[step * 2 + owner, pl.ds(192, 192), cols] = second[owner * 192:(owner + 1) * 192]
    pltpu.make_async_copy(held_grads.at[pair], gexp.at[pair], sems.at[step]).start()

    for k in range(3):
        @pl.when(step == k)
        def _(k=k):
            cols = pl.ds(k * 768, 768)
            grad = mm(both(c_nin), jnp.concatenate([b_gp[0, :, cols], b_gp[1, :, cols]], axis=0), TN).astype(LOW)
            for owner in range(16):
                gden[owner, pl.ds(32, 48), cols] = grad[owner * 48:(owner + 1) * 48]

    @pl.when(step == 3)
    def _():
        grad = mm(both(c_mix), both(b_ga), TN).astype(LOW)
        for owner in range(16):
            for k in range(3):
                at = owner * 48 + k * 16
                gden[owner, pl.ds(16, 16), pl.ds(k * 768, 768)] = grad[at:at + 16]

    @pl.when(step == 4)
    def _():
        router = mm(both(b_gl), both(c_nrm), TN)[:8]
        small = jnp.concatenate([router, b_norm[0] + b_norm[1]], axis=0).astype(LOW)
        for owner in range(16):
            gden[owner, pl.ds(0, 16), pl.ds(0, 768)] = small
            gden[owner, pl.ds(0, 16), pl.ds(768, 1536)] = jnp.zeros((16, 1536), LOW)

    @pl.when(step == SPANS - 1)
    def _():
        for k in range(SPANS):
            done = pl.ds(k * 2, 2)
            pltpu.make_async_copy(held_grads.at[done], gexp.at[done], sems.at[k]).wait()


def weight_grads(caches, backs):
    _, _, c_nin, _, c_mix, _, c_nrm, _, c_slot, _, c_hid, _ = caches
    _, b_gres, b_gpre, b_ga, b_gp, b_gl, b_norm = backs
    operands = [c_nin, c_mix, c_nrm, c_slot, c_hid, b_gres, b_gpre, b_ga, b_gp, b_gl, b_norm]

    def spec(shape):
        if shape[-1] == 3072:
            return pl.BlockSpec((2, shape[1], 384), lambda j: (0, 0, j))
        return pl.BlockSpec(shape, lambda j: (0, 0, 0))

    return pl.pallas_call(
        weight_kernel,
        out_shape=[
            jax.ShapeDtypeStruct((16, 384, 2304), LOW),
            jax.ShapeDtypeStruct((16, 80, 2304), LOW),
        ],
        grid=(SPANS,),
        in_specs=[spec(array.shape) for array in operands],
        out_specs=[
            pl.BlockSpec(memory_space=pl.ANY),
            pl.BlockSpec((16, 80, 2304), lambda j: (0, 0, 0)),
        ],
        scratch_shapes=[pltpu.VMEM((16, 384, 2304), LOW), pltpu.SemaphoreType.DMA((SPANS,))],
        compiler_params=pltpu.CompilerParams(vmem_limit_bytes=60 * 1024 * 1024),
    )(*operands)


def spread_kernel(total, g_in, g_out, g_qkv, g_proj, small):
    for e in range(3):
        cols = pl.ds(e * 768, 768)
        g_in[0, e] = total[pl.ds(80, 192), cols].astype(F32)
        g_out[0, e] = total[pl.ds(272, 192), cols].astype(F32)
        g_proj[0, pl.ds(e * 16, 16), :] = total[pl.ds(16, 16), cols].astype(F32)
    g_qkv[0] = total[pl.ds(32, 48), :].astype(F32)
    small[...] = total[pl.ds(0, 16), pl.ds(0, 768)].astype(F32)


def spread(total):
    shapes = [(1, 3, 192, 768), (1, 3, 192, 768), (1, 48, 2304), (1, 48, 768), (16, 768)]
    return pl.pallas_call(
        spread_kernel,
        out_shape=[jax.ShapeDtypeStruct(shape, F32) for shape in shapes],
        compiler_params=pltpu.CompilerParams(vmem_limit_bytes=60 * 1024 * 1024),
    )(total)


def hop_kernel(value, out, send, recv):
    peer = {"section": 1 - lax.axis_index("section")}
    greet([peer])
    cp = pltpu.make_async_remote_copy(
        src_ref=value, dst_ref=out, send_sem=send, recv_sem=recv, device_id=peer, device_id_type=MESH
    )
    cp.start()
    cp.wait()


def swap_sections(value):
    return pl.pallas_call(
        hop_kernel,
        out_shape=jax.ShapeDtypeStruct(value.shape, value.dtype),
        in_specs=[pl.BlockSpec(memory_space=pl.ANY)],
        out_specs=pl.BlockSpec(memory_space=pl.ANY),
        scratch_shapes=[pltpu.SemaphoreType.DMA(()), pltpu.SemaphoreType.DMA(())],
        compiler_params=pltpu.CompilerParams(collective_id=2, has_side_effects=True),
    )(value)


def local(
    inputs, cotangent, routes, norm_gain, norm_offset, w_qkv, w_proj, w_router, experts_in, experts_out
):
    at = lax.axis_index("section").astype(jnp.int32).reshape(1)
    ahead = (lambda at: 0, lambda at: 1 - at[0], lambda at: 1)
    back = (lambda at: 0, lambda at: at[0], lambda at: 1)
    small = jnp.concatenate([w_router[0], norm_gain[0].T, norm_offset[0].T], axis=1)
    own = jnp.concatenate(
        [
            jnp.concatenate([experts_in[0, :, e] for e in range(3)], axis=1),
            jnp.concatenate([experts_out[0, :, e] for e in range(3)], axis=1),
            w_qkv[0],
            w_proj[0].reshape(3, 16, 768).transpose(1, 0, 2).reshape(16, 2304),
            jnp.pad(small.reshape(16, 21), ((0, 0), (0, 2283))),
        ],
        axis=0,
    )
    every = gather(own, 208).reshape(16, 464, 2304)
    small = every[:, 448:, :21].reshape(768, 7)
    router = jnp.pad(small[:, :3], ((0, 0), (0, LANES - 3)))
    norms = jnp.pad(small[:, 3:].T.astype(F32), ((0, 4), (0, 0)))
    pad = ((0, 0), (0, TOKENS - 197), (0, 0))
    inputs = jnp.pad(inputs[:, 0], pad)
    cotangent = jnp.pad(cotangent[:, 0], pad)
    routes = jnp.pad(routes[0, :, 0], ((0, 0), (0, TOKENS - 197), (0, LANES - 2)), constant_values=-1)
    received = jnp.zeros((TOKENS, 768), LOW)
    caches = None
    for tick in range(3):
        sent, caches = forward_tick(ahead[tick], at, inputs, received, routes, every, router, norms, caches)
        if tick < 2:
            received = swap_sections(sent)
    returned = jnp.zeros((TOKENS, 768), LOW)
    backs = None
    for tick in range(3):
        sent, backs = backward_tick(back[tick], at, cotangent, returned, routes, every, router, norms, caches, backs)
        if tick < 2:
            returned = swap_sections(sent)
    gexp, gden = weight_grads(caches, backs)
    total = reduce_grads(gexp.reshape(2, 4, 2, 384, 2304), gden.reshape(2, 4, 2, 80, 2304))
    g_in, g_out, g_qkv, g_proj, small = spread(total)
    mine = lax.dynamic_slice_in_dim(small, lax.axis_index("shard") * 48, 48, axis=1)
    return (
        caches[0][None, :, None],
        backs[0][None, :, None],
        mine[8:10][None],
        mine[10:12][None],
        g_qkv,
        g_proj,
        mine[:3].T[None],
        g_in.transpose(0, 2, 1, 3),
        g_out.transpose(0, 2, 1, 3),
    )


def solution(mesh):
    return jax.shard_map(
        local,
        mesh=mesh,
        in_specs=(
            P(None, ("replica", "shard"), None, None),
            P(None, ("replica", "shard"), None, None),
            P("section", None, ("replica", "shard"), None, None),
            P("section", None, "shard"),
            P("section", None, "shard"),
            P("section", "shard", None),
            P("section", "shard", None),
            P("section", "shard", None),
            P("section", "shard", None, None),
            P("section", "shard", None, None),
        ),
        out_specs=(
            P("section", None, ("replica", "shard"), None, None),
            P("section", None, ("replica", "shard"), None, None),
            P("section", None, "shard"),
            P("section", None, "shard"),
            P("section", "shard", None),
            P("section", "shard", None),
            P("section", "shard", None),
            P("section", "shard", None, None),
            P("section", "shard", None, None),
        ),
        check_vma=False,
    )
```
